512 devices in a mesh: inst: 16 (over x, y_hi), dom: 32 (over z, y_lo, core).
Axes of the slice: x: 4, y: 8 (y_hi: 4, y_lo: 2; y = y_hi * 2 + y_lo), z: 8, core: 2. Of those that a mesh axis runs over, the one named last changes fastest.
Arguments:
- flow_state: float32 [16, 5, 8192, 128], P('inst', None, 'dom'), may hold values from -6 to 6
- wave_speed: float32 [5], replicated, may hold values from 0.5 to 1.5
- frequency: float32 [1], replicated, may hold values from 0.05 to 0.3
- time_weights: float32 [16], replicated, may hold values from 0.05 to 0.5
- phase_shift: int32 [16], replicated, may hold values from 0 to 1023
- donor_part: int32 [1024, 4], replicated, may hold values from 0 to 31, as said below
- donor_block: int32 [1024, 4], replicated, may hold values from 0 to 255
- donor_count: int32 [1024], replicated, may hold values from 1 to 4
- donor_weight: float32 [1024, 4], replicated, may hold values from 0.1 to 1
Outputs:
- residual: float32 [16, 5, 8192, 128], P('inst', None, 'dom')
- interface_rows: float32 [16, 5, 1024, 128], P('inst', None, 'dom')
The draws below stay inside these ranges and needn't reach their ends.
Inputs may be any that keep to these rules, and one draw needn't show every extreme that they name: `donor_part`: among the 128 entries of the rows of one partition, every partition appears exactly 4 times, padding entries included. Entries k >= donor_count[r] of row r are padding and carry no weight.
All inputs are finite; a program needn't handle non-finite values.
Results may differ from the reference program's by a relative error of at most 0.00007.
Values sent between devices are 32-bit elements; how exact they have to be, the bound alone decides.
A program may use at most 192 MiB of HBM per device.

```python
import jax
import jax.numpy as jnp
from jax import lax

V = 5
NI = 16
GX = 256
GZ = 128
R_DEV = 32
K = 4
NX = 8192
ROWS = 1024


def draw_donor_part(key, part):
    key = jax.random.fold_in(key, 11)
    partitions = ROWS // R_DEV
    key_list = jax.random.split(key, partitions)
    orders = jax.vmap(lambda key_one: jax.random.permutation(key_one, R_DEV * K))(key_list)
    return (orders % partitions).reshape(ROWS, K).astype(jnp.int32)


def plant(array, rng, least, high):
    spot = [jax.random.randint(jax.random.fold_in(rng, axis), (), 0, length) for axis, length in enumerate(array.shape)]
    longest = array.shape.index(max(array.shape))
    beside = spot[:longest] + [(spot[longest] + 1) % array.shape[longest]] + spot[longest + 1:]
    return array.at[tuple(spot)].set(least).at[tuple(beside)].set(high)


def steps_of(own_key, extent, cuts, smallest, largest):
    level, own = 1.0, jax.random.fold_in(own_key, 6)
    for dim, blocks in cuts:
        draws = jnp.exp(jax.random.uniform(jax.random.fold_in(own, dim), (blocks,), jnp.float32, smallest / len(cuts), largest / len(cuts)))
        level = level * jnp.repeat(draws, extent[dim] // blocks).reshape([-1 if axis == dim else 1 for axis in range(len(extent))])
    return level


def gaussian(own_key, extent, spread, limit, cuts=(), kind=jnp.bfloat16):
    result = jax.random.normal(own_key, extent, jnp.float32) * spread
    if len(cuts) > 0:
        result = steps_of(own_key, extent, cuts, -0.22, 0.18) * result
    return jnp.clip(result, min=-limit, max=limit).astype(kind)


def setup_inputs(seed: int = 0) -> dict:
    key_of = jax.random.split(jax.random.key(seed), 10)
    flow_state = gaussian(key_of[0], (NI, V, NX, GZ), 1.0, 6.0, ((0, 16), (2, 32)), jnp.float32)
    wave_speed = jnp.clip(jax.random.uniform(key_of[1], (V,), jnp.float32, 0.5, 1.5), 0.5, 1.5)
    frequency = jnp.clip(jax.random.uniform(key_of[2], (1,), jnp.float32, 0.05, 0.3), 0.05, 0.3)
    time_weights = jnp.clip(jax.random.uniform(key_of[3], (NI,), jnp.float32, 0.05, 0.5), 0.05, 0.5)
    phase_shift = plant(jax.random.randint(key_of[4], (NI,), 0, 64 * NI), jax.random.fold_in(key_of[4], 1), 0, (64 * NI) - 1).astype(jnp.int32)
    donor_part = draw_donor_part(jax.random.fold_in(key_of[9], 71), 0)
    donor_block = plant(jax.random.randint(key_of[6], (ROWS, K), 0, GX), jax.random.fold_in(key_of[6], 1), 0, GX - 1).astype(jnp.int32)
    donor_count = plant(jax.random.randint(key_of[7], (ROWS,), 1, K + 1), jax.random.fold_in(key_of[7], 1), 1, K).astype(jnp.int32)
    donor_weight = jnp.clip(jax.random.uniform(key_of[8], (ROWS, K), jnp.float32, 0.1, 1.0), 0.1, 1.0)
    return {"flow_state": flow_state, "wave_speed": wave_speed, "frequency": frequency, "time_weights": time_weights, "phase_shift": phase_shift, "donor_part": donor_part, "donor_block": donor_block, "donor_count": donor_count, "donor_weight": donor_weight}


highest = lax.Precision.HIGHEST


def time_table(length):
    indices = jnp.arange(length, dtype=jnp.int32)
    offset = indices[:, None] - indices[None, :]
    safe_off = jnp.where(offset == 0, 1, offset).astype(jnp.float32)
    signs = jnp.where(offset % 2 == 0, 1.0, -1.0).astype(jnp.float32)
    values_table = 0.5 * signs / jnp.tan(jnp.pi * safe_off / length)
    values_table = jnp.where(offset == 0, -2.0, values_table) + 2.0 / length
    return values_table.astype(jnp.float32)


def reference(flow_state, wave_speed, frequency, time_weights, phase_shift, donor_part, donor_block, donor_count, donor_weight):
    spectral = time_table(NI)
    derivative = jnp.einsum('im,mvxz->ivxz', spectral, flow_state, precision=highest)
    padded = jnp.pad(flow_state, ((0, 0), (0, 0), (1, 1), (0, 0)))
    upper_z = jnp.roll(flow_state, -1, 3)
    lower_z = jnp.roll(flow_state, 1, 3)
    laplace = padded[:, :, 2:] + padded[:, :, :-2] + upper_z + lower_z - 4.0 * flow_state
    advect = wave_speed[None, :, None, None] * (upper_z - lower_z) * 0.5
    live_mask = (jnp.arange(K, dtype=jnp.int32)[None, :] < donor_count[:, None]).astype(jnp.float32)
    normed = donor_weight * live_mask
    normed = normed / jnp.sum(normed, axis=1, keepdims=True)
    row_index = donor_part * GX + donor_block

    def remap_one(single):
        picked = single[:, row_index]
        return jnp.einsum('vrkz,rk->vrz', picked, normed, precision=highest)

    mapped = lax.map(remap_one, flow_state)
    columns = (jnp.arange(NI, dtype=jnp.int32)[None, :] - phase_shift[:, None]) % NI
    weight_matrix = time_weights[columns]
    interface_rows = jnp.einsum('im,mvrz->ivrz', weight_matrix, mapped, precision=highest)
    partitions = NX // GX
    local_rows = flow_state.reshape(NI, V, partitions, GX, GZ)[:, :, :, :R_DEV]
    penalty = interface_rows.reshape(NI, V, partitions, R_DEV, GZ) - local_rows
    penalty = jnp.pad(penalty, ((0, 0), (0, 0), (0, 0), (0, GX - R_DEV), (0, 0))).reshape(NI, V, NX, GZ)
    residual = 0.25 * laplace - advect - frequency[0] * derivative + 0.5 * penalty
    return residual, interface_rows
```

```python
import functools

import jax
import jax.numpy as jnp
import numpy as np
from jax import lax
from jax.experimental import pallas as pl
from jax.experimental.pallas import tpu as pltpu
from jax.sharding import PartitionSpec as P

HIGHEST = lax.Precision.HIGHEST
MESH = pl.DeviceIdType.MESH
GROUPS = ((0, 2), (2, 4), (4, 5))


def spectral_line(length):
    j = np.arange(length)
    safe = np.where(j == 0, 1, j)
    line = 0.5 * np.where(j % 2 == 0, 1.0, -1.0) / np.tan(np.pi * safe / length)
    return np.where(j == 0, -2.0, line) + 2.0 / length


def iota(shape, dim):
    return lax.broadcasted_iota(jnp.int32, shape, dim)


def send_table(part_ref, block_ref, dom, ndom, rows, donors):
    lanes = 128
    chunks = ndom * rows // lanes
    parts = jnp.concatenate([part_ref[:, lanes * g : lanes * (g + 1)] for g in range(chunks)], axis=0)
    blocks = jnp.concatenate([block_ref[:, lanes * g : lanes * (g + 1)] for g in range(chunks)], axis=0)
    count = chunks * donors
    cap = rows * donors // ndom
    per = lanes // rows
    wanted = parts == dom
    ones = jnp.where(wanted, 1.0, 0.0)
    a, b = iota((lanes, lanes), 0), iota((lanes, lanes), 1)
    same = (a // rows) == (b // rows)
    before = jnp.where(same & (a < b), 1.0, 0.0)
    whole = jnp.where(same, 1.0, 0.0)
    ra, rb = iota((count, count), 0), iota((count, count), 1)
    lower = jnp.where(((ra // donors) == (rb // donors)) & (rb < ra), 1.0, 0.0)
    dot = functools.partial(jnp.dot, preferred_element_type=jnp.float32)
    rank = dot(ones, before) + dot(lower, dot(ones, whole))
    total = jnp.zeros((count, lanes), jnp.float32)
    values = blocks.astype(jnp.float32)
    for c in range(cap):
        picked = jnp.where(wanted & (rank == float(c)), values, 0.0)
        spread = jnp.where((b % (per * cap)) == (a // rows) * cap + c, 1.0, 0.0)
        total = total + dot(picked, spread)
    row, lane = iota((count, lanes), 0), iota((count, lanes), 1)
    line = jnp.sum(
        jnp.where((lane // (per * cap)) == (row // donors), total, 0.0), axis=0, keepdims=True
    )
    return jnp.transpose(jnp.broadcast_to(line, (lanes, lanes)))


def weight_table(part_ref, weight_ref, count_ref, dom, ndom, rows, donors):
    lanes = 128
    per = lanes // rows
    cap = rows * donors // ndom
    at = pl.ds(pl.multiple_of((dom // per) * lanes, lanes), lanes)
    own = jnp.concatenate(
        [
            part_ref[:, at].astype(jnp.float32),
            weight_ref[:, at],
            jnp.broadcast_to(count_ref[:, at].astype(jnp.float32), (8, lanes)),
        ],
        axis=0,
    )
    a, b = iota((lanes, lanes), 0), iota((lanes, lanes), 1)
    pick = jnp.where(a == (dom % per) * rows + b % rows, 1.0, 0.0)
    own = jnp.dot(own, pick, precision=HIGHEST, preferred_element_type=jnp.float32)
    row, lane = iota((donors, lanes), 0), iota((donors, lanes), 1)
    mine = (lane // rows) == row
    part = jnp.sum(jnp.where(mine, own[:donors], 0.0), axis=0, keepdims=True)
    live = mine & (row.astype(jnp.float32) < own[2 * donors : 3 * donors])
    weight = jnp.sum(jnp.where(live, own[donors : 2 * donors], 0.0), axis=0, keepdims=True)
    part_row = jnp.broadcast_to(part, (lanes, lanes))
    part_col = jnp.transpose(part_row)
    rank = jnp.sum(jnp.where((part_row == part_col) & (a < b), 1.0, 0.0), axis=0, keepdims=True)
    slot_col = jnp.transpose(jnp.broadcast_to(part * cap + rank, (lanes, lanes)))
    weight_col = jnp.transpose(jnp.broadcast_to(weight, (lanes, lanes)))
    spread = jnp.where(slot_col == b.astype(jnp.float32), weight_col, 0.0)
    top = sum(spread[rows * k : rows * (k + 1)] for k in range(donors))
    bottom = sum(weight_col[rows * k : rows * (k + 1)] for k in range(donors))
    return top / bottom


def kernel(
    ninst,
    ndom,
    x,
    speed,
    freq,
    time_weights,
    shift,
    part,
    block,
    weight,
    count,
    res,
    ghost,
    sbuf,
    rbuf,
    fbuf,
    obuf,
    back,
    mbuf,
    mrec,
    gout,
    gback,
    hsend,
    hrecv,
    wtab,
    d_send,
    d_recv,
    f_send,
    f_recv,
    b_send,
    b_recv,
    m_send,
    m_recv,
    g_send,
    g_recv,
    h_send,
    h_recv,
):
    nv, cells, pitch = x.shape
    rows = ghost.shape[1]
    donors = part.shape[0]
    cap = rows * donors // ndom
    cut = cells // ninst
    fine = rows // ninst
    me, dom = lax.axis_index("inst"), lax.axis_index("dom")

    def inst_of(k):
        return lax.rem(me + k, ninst)

    def dom_of(k):
        return lax.rem(dom + k, ndom)

    def own_rows(i):
        return pl.ds(pl.multiple_of(i * cut, cut), cut)

    def remote(src, dst, send, recv, to):
        return pltpu.make_async_remote_copy(
            src_ref=src, dst_ref=dst, send_sem=send, recv_sem=recv, device_id=to, device_id_type=MESH
        )

    def donor_copy(k):
        to = dom_of(k)
        return remote(sbuf.at[to], rbuf.at[dom], d_send.at[k], d_recv.at[ndom - k], (me, to))

    def donor_arrival(k):
        return remote(sbuf.at[0], rbuf.at[dom_of(k)], d_send.at[k], d_recv.at[k], (me, dom_of(k)))

    def forward_copy(g, k):
        v0, v1 = GROUPS[g]
        to = inst_of(k)
        return remote(
            x.at[v0:v1, own_rows(to)],
            fbuf.at[ninst - k, v0:v1],
            f_send.at[g, k],
            f_recv.at[g, ninst - k],
            (to, dom),
        )

    def forward_arrival(g, k):
        v0, v1 = GROUPS[g]
        return remote(
            x.at[v0:v1, own_rows(me)], fbuf.at[k, v0:v1], f_send.at[g, k], f_recv.at[g, k], (inst_of(k), dom)
        )

    def back_copy(g, k):
        v0, v1 = GROUPS[g]
        return remote(
            obuf.at[k, v0:v1],
            back.at[v0:v1, own_rows(me)],
            b_send.at[g, k],
            b_recv.at[g, ninst - k],
            (inst_of(k), dom),
        )

    def back_arrival(g, k):
        v0, v1 = GROUPS[g]
        return remote(
            obuf.at[k, v0:v1], back.at[v0:v1, own_rows(inst_of(k))], b_send.at[g, k], b_recv.at[g, k], (inst_of(k), dom)
        )

    def mapped_copy(k):
        to = inst_of(k)
        return remote(mbuf.at[to], mrec.at[ninst - k], m_send.at[k], m_recv.at[ninst - k], (to, dom))

    def mapped_arrival(k):
        return remote(mbuf.at[0], mrec.at[k], m_send.at[k], m_recv.at[k], (inst_of(k), dom))

    def ghost_copy(k):
        return remote(gout.at[k], gback.at[me], g_send.at[k], g_recv.at[ninst - k], (inst_of(k), dom))

    def ghost_arrival(k):
        return remote(gout.at[k], gback.at[inst_of(k)], g_send.at[k], g_recv.at[k], (inst_of(k), dom))

    def halo_copy(side):
        to = dom_of(1 if side == 0 else ndom - 1)
        return remote(hsend.at[side], hrecv.at[side], h_send.at[side], h_recv.at[side], (me, to))

    def each(count, act):
        def step(k, carry):
            act(k)
            return carry

        lax.fori_loop(1, count, step, 0)

    barrier = pltpu.get_barrier_semaphore()
    each(ndom, lambda k: pl.semaphore_signal(barrier, inc=1, device_id=(me, dom_of(k)), device_id_type=MESH))
    each(ninst, lambda k: pl.semaphore_signal(barrier, inc=1, device_id=(inst_of(k), dom), device_id_type=MESH))

    column = send_table(part, block, dom, ndom, rows, donors)
    lane = iota(column.shape, 1).astype(jnp.float32)
    chosen = jnp.concatenate(
        [jnp.where(column == lane + float(s), 1.0, 0.0) for s in range(0, cells, 128)], axis=1
    )
    for v in range(nv):
        out = jnp.dot(chosen, x[v], precision=HIGHEST, preferred_element_type=jnp.float32)
        for q in range(ndom):
            sbuf[q, v] = out[q * cap : (q + 1) * cap]
        hsend[0, v] = x[v, cells - 1 :, :]
        hsend[1, v] = x[v, :1, :]

    pl.semaphore_wait(barrier, ndom - 1 + ninst - 1)
    halo_copy(0).start()
    halo_copy(1).start()
    each(ndom, lambda k: donor_copy(k).start())
    for g in range(len(GROUPS)):
        each(ninst, lambda k: forward_copy(g, k).start())

    rbuf[dom] = sbuf[dom]
    for v in range(nv):
        fbuf[0, v] = x[v, own_rows(me), :]

    def weights_of(target, carry):
        phase = shift[inst_of(target)]
        for k in range(ninst):
            wtab[target * ninst + k] = time_weights[jnp.bitwise_and(me + k - phase, ninst - 1)]
        return carry

    lax.fori_loop(0, ninst, weights_of, 0)
    table = weight_table(part, weight, count, dom, ndom, rows, donors)

    halo_copy(0).wait_recv()
    halo_copy(1).wait_recv()
    edge = iota((cells, pitch), 0)
    for v in range(nv):
        u = x[v]
        low = jnp.where(dom == 0, 0.0, hrecv[0, v])
        high = jnp.where(dom == ndom - 1, 0.0, hrecv[1, v])
        below = jnp.where(edge == 0, low, pltpu.roll(u, 1, 0))
        above = jnp.where(edge == cells - 1, high, pltpu.roll(u, cells - 1, 0))
        upper = pltpu.roll(u, pitch - 1, 1)
        lower = pltpu.roll(u, 1, 1)
        base = 0.25 * (above + below + upper + lower - 4.0 * u) - speed[v] * (upper - lower) * 0.5
        res[v] = base
        res[v, :rows] = base[:rows] - 0.5 * u[:rows]

    line = spectral_line(ninst)
    half = ninst // 2
    even = [float(np.float32(0.5 * (line[j] + line[j + half]))) for j in range(half)]
    odd = [float(np.float32(0.5 * (line[j] - line[j + half]))) for j in range(half)]
    scale = -freq[0]

    def mix(g):
        v0, v1 = GROUPS[g]
        each(ninst, lambda k: forward_arrival(g, k).wait_recv())

        def tile(t, carry):
            v = v0 + t // (cut // 8)
            r = pl.multiple_of((t % (cut // 8)) * 8, 8)
            f = [fbuf[k, v, pl.ds(r, 8), :] for k in range(ninst)]
            e = [scale * (f[k] + f[k + half]) for k in range(half)]
            o = [scale * (f[k] - f[k + half]) for k in range(half)]
            for target in range(half):
                total_e = total_o = None
                for k in range(half):
                    j = target - k
                    ce = even[j % half]
                    co = odd[j] if j >= 0 else -odd[j + half]
                    total_e = ce * e[k] if total_e is None else total_e + ce * e[k]
                    total_o = co * o[k] if total_o is None else total_o + co * o[k]
                if target == 0:
                    back[v, pl.ds(pl.multiple_of(me * cut + r, 8), 8), :] = total_e + total_o
                else:
                    obuf[target, v, pl.ds(r, 8), :] = total_e + total_o
                obuf[target + half, v, pl.ds(r, 8), :] = total_e - total_o
            return carry

        lax.fori_loop(0, (v1 - v0) * (cut // 8), tile, 0)
        each(ninst, lambda k: back_copy(g, k).start())

    def remap():
        each(ndom, lambda k: donor_arrival(k).wait_recv())
        for v in range(nv):
            arrived = jnp.concatenate([rbuf[p, v] for p in range(ndom)], axis=0)
            rows_v = jnp.dot(table, arrived, precision=HIGHEST, preferred_element_type=jnp.float32)
            for s in range(ninst):
                mbuf[s, fine * v : fine * (v + 1)] = rows_v[fine * s : fine * (s + 1)]
        each(ninst, lambda k: mapped_copy(k).start())
        mrec[0] = mbuf[me]

    def interpolate():
        each(ninst, lambda k: mapped_arrival(k).wait_recv())

        def one(target, carry):
            total = wtab[target * ninst] * mrec[0]
            for k in range(1, ninst):
                total = total + wtab[target * ninst + k] * mrec[k]
            gout[target] = total
            return carry

        lax.fori_loop(0, ninst, one, 0)
        each(ninst, lambda k: ghost_copy(k).start())
        gback[me] = gout[0]

    remap()
    mix(0)
    mix(1)
    interpolate()
    mix(2)

    for g, (v0, v1) in enumerate(GROUPS):
        each(ninst, lambda k: back_arrival(g, k).wait_recv())
        for v in range(v0, v1):
            res[v] = res[v] + back[v]
    each(ninst, lambda k: ghost_arrival(k).wait_recv())
    for v in range(nv):
        full = jnp.concatenate([gback[s, fine * v : fine * (v + 1)] for s in range(ninst)], axis=0)
        ghost[v] = full
        res[v, :rows] = res[v, :rows] + 0.5 * full

    halo_copy(0).wait_send()
    halo_copy(1).wait_send()
    each(ndom, lambda k: donor_copy(k).wait_send())
    for g in range(len(GROUPS)):
        each(ninst, lambda k: forward_copy(g, k).wait_send())
        each(ninst, lambda k: back_copy(g, k).wait_send())
    each(ninst, lambda k: mapped_copy(k).wait_send())
    each(ninst, lambda k: ghost_copy(k).wait_send())


def solution(mesh):
    ninst, ndom = mesh.shape["inst"], mesh.shape["dom"]

    def body(flow_state, speed, freq, time_weights, shift, part, block, count, weight):
        x = flow_state[0]
        nv, cells, pitch = x.shape
        rows = part.shape[0] // ndom
        donors = part.shape[1]
        cap = rows * donors // ndom
        cut = cells // ninst
        fine = rows // ninst
        groups = len(GROUPS)
        vmem = pl.BlockSpec(memory_space=pltpu.VMEM)
        smem = pl.BlockSpec(memory_space=pltpu.SMEM)
        f32 = jnp.float32
        dma = pltpu.SemaphoreType.DMA
        res, ghost = pl.pallas_call(
            functools.partial(kernel, ninst, ndom),
            out_shape=(
                jax.ShapeDtypeStruct((nv, cells, pitch), f32),
                jax.ShapeDtypeStruct((nv, rows, pitch), f32),
            ),
            in_specs=[vmem, smem, smem, smem, smem, vmem, vmem, vmem, vmem],
            out_specs=(vmem, vmem),
            scratch_shapes=[
                pltpu.VMEM((ndom, nv, cap, pitch), f32),
                pltpu.VMEM((ndom, nv, cap, pitch), f32),
                pltpu.VMEM((ninst, nv, cut, pitch), f32),
                pltpu.VMEM((ninst, nv, cut, pitch), f32),
                pltpu.VMEM((nv, cells, pitch), f32),
                pltpu.VMEM((ninst, nv * fine, pitch), f32),
                pltpu.VMEM((ninst, nv * fine, pitch), f32),
                pltpu.VMEM((ninst, nv * fine, pitch), f32),
                pltpu.VMEM((ninst, nv * fine, pitch), f32),
                pltpu.VMEM((2, nv, 1, pitch), f32),
                pltpu.VMEM((2, nv, 1, pitch), f32),
                pltpu.SMEM((ninst * ninst,), f32),
                dma((ndom,)),
                dma((ndom,)),
                dma((groups, ninst)),
                dma((groups, ninst)),
                dma((groups, ninst)),
                dma((groups, ninst)),
                dma((ninst,)),
                dma((ninst,)),
                dma((ninst,)),
                dma((ninst,)),
                dma((2,)),
                dma((2,)),
            ],
            compiler_params=pltpu.CompilerParams(
                collective_id=0, has_side_effects=True, vmem_limit_bytes=40 << 20
            ),
            name="harmonic_residual",
        )(x, speed, freq, time_weights, shift, part.T, block.T, weight.T, count[None])
        return res[None], ghost[None]

    in_specs = (P("inst", None, "dom", None), P(), P(), P(), P(), P(), P(), P(), P())
    out_specs = (P("inst", None, "dom", None), P("inst", None, "dom", None))
    return jax.shard_map(body, mesh=mesh, in_specs=in_specs, out_specs=out_specs, check_vma=False)
```

```python
import functools

import jax
import jax.numpy as jnp
import numpy as np
from jax import lax
from jax.experimental import pallas as pl
from jax.experimental.pallas import tpu as pltpu
from jax.sharding import PartitionSpec as P

HIGHEST = lax.Precision.HIGHEST
VMEM = 56 << 20
MESH = pl.DeviceIdType.MESH
GROUPS = ((0, 2), (2, 4), (4, 5))
ORDER = (2, 10, 6, 14, 9, 5, 11, 7, 1, 13, 3, 15, 8, 4, 12)


def spectral_line(length):
    j = np.arange(length)
    safe = np.where(j == 0, 1, j)
    line = 0.5 * np.where(j % 2 == 0, 1.0, -1.0) / np.tan(np.pi * safe / length)
    return np.where(j == 0, -2.0, line) + 2.0 / length


def iota(shape, dim):
    return lax.broadcasted_iota(jnp.int32, shape, dim)


def send_table(part_ref, block_ref, dom, ndom, rows, donors):
    lanes = 128
    chunks = ndom * rows // lanes
    parts = jnp.concatenate([part_ref[:, lanes * g : lanes * (g + 1)] for g in range(chunks)], axis=0)
    blocks = jnp.concatenate([block_ref[:, lanes * g : lanes * (g + 1)] for g in range(chunks)], axis=0)
    count = chunks * donors
    cap = rows * donors // ndom
    per = lanes // rows
    wanted = parts == dom
    ones = jnp.where(wanted, 1.0, 0.0)
    a, b = iota((lanes, lanes), 0), iota((lanes, lanes), 1)
    same = (a // rows) == (b // rows)
    before = jnp.where(same & (a < b), 1.0, 0.0)
    whole = jnp.where(same, 1.0, 0.0)
    ra, rb = iota((count, count), 0), iota((count, count), 1)
    lower = jnp.where(((ra // donors) == (rb // donors)) & (rb < ra), 1.0, 0.0)
    dot = functools.partial(jnp.dot, preferred_element_type=jnp.float32)
    rank = dot(ones, before) + dot(lower, dot(ones, whole))
    total = jnp.zeros((count, lanes), jnp.float32)
    values = blocks.astype(jnp.float32)
    for c in range(cap):
        picked = jnp.where(wanted & (rank == float(c)), values, 0.0)
        group = a // rows
        spread = jnp.where((b % (per * cap)) == ((group % 2) * 2 + group // 2) * cap + c, 1.0, 0.0)
        total = total + dot(picked, spread)
    row, lane = iota((count, lanes), 0), iota((count, lanes), 1)
    line = jnp.sum(
        jnp.where((lane // (per * cap)) == (row // donors), total, 0.0), axis=0, keepdims=True
    )
    return jnp.transpose(jnp.broadcast_to(line, (lanes, lanes)))


def weight_table(part_ref, weight_ref, count_ref, dom, side, ndom, rows, donors):
    lanes = 128
    per = lanes // rows
    cap = rows * donors // ndom
    at = pl.ds(pl.multiple_of((dom // per) * lanes, lanes), lanes)
    own = jnp.concatenate(
        [
            part_ref[:, at].astype(jnp.float32),
            weight_ref[:, at],
            jnp.broadcast_to(count_ref[:, at].astype(jnp.float32), (8, lanes)),
        ],
        axis=0,
    )
    a, b = iota((lanes, lanes), 0), iota((lanes, lanes), 1)
    pick = jnp.where(a == (dom % per) * rows + b % rows, 1.0, 0.0)
    own = jnp.dot(own, pick, precision=HIGHEST, preferred_element_type=jnp.float32)
    row, lane = iota((donors, lanes), 0), iota((donors, lanes), 1)
    mine = (lane // rows) == row
    part = jnp.sum(jnp.where(mine, own[:donors], 0.0), axis=0, keepdims=True)
    live = mine & (row.astype(jnp.float32) < own[2 * donors : 3 * donors])
    weight = jnp.sum(jnp.where(live, own[donors : 2 * donors], 0.0), axis=0, keepdims=True)
    part_row = jnp.broadcast_to(part, (lanes, lanes))
    part_col = jnp.transpose(part_row)
    rank = jnp.sum(jnp.where((part_row == part_col) & (a < b), 1.0, 0.0), axis=0, keepdims=True)
    named = part.astype(jnp.int32)
    site = (named // 4) * 2 + named % 2
    slot = (site * 2 + (dom // 2) % 2).astype(jnp.float32) * cap + rank
    slot = jnp.where((named // 2) % 2 == side, slot, -1.0)
    slot_col = jnp.transpose(jnp.broadcast_to(slot, (lanes, lanes)))
    weight_col = jnp.transpose(jnp.broadcast_to(weight, (lanes, lanes)))
    spread = jnp.where(slot_col == b.astype(jnp.float32), weight_col, 0.0)
    top = sum(spread[rows * k : rows * (k + 1)] for k in range(donors))
    bottom = sum(weight_col[rows * k : rows * (k + 1)] for k in range(donors))
    return top / bottom


def kernel(
    ninst,
    ndom,
    x_in,
    speed_in,
    freq_in,
    time_weights_in,
    shift_in,
    part_in,
    block_in,
    weight_in,
    count_in,
    res_out,
    ghost_out,
    x,
    speed,
    freq,
    time_weights,
    shift,
    part,
    block,
    weight,
    count,
    loads,
    res,
    ghost,
    stores,
    sbuf,
    rbuf,
    fbuf,
    obuf,
    back,
    psend,
    precv,
    mbuf,
    mrec,
    gout,
    gback,
    hsend,
    hrecv,
    wtab,
    d_send,
    d_recv,
    f_send,
    f_recv,
    b_send,
    b_recv,
    p_send,
    p_recv,
    m_send,
    m_recv,
    g_send,
    g_recv,
    h_send,
    h_recv,
):
    nv, cells, pitch = x.shape
    rows = ghost.shape[1]
    donors = part.shape[0]
    cap = rows * donors // ndom
    cut = cells // ninst
    fine = rows // ninst
    me, dom = lax.axis_index("inst"), lax.axis_index("dom")

    def inst_of(k):
        return lax.rem(me + k, ninst)

    def dom_of(k):
        return lax.rem(dom + k, ndom)

    nsite = ndom // 2
    side = (dom // 2) % 2
    site = (dom // 4) * 2 + dom % 2
    mate = dom + 2 - 4 * side

    def site_of(k):
        return lax.rem(site + k, nsite)

    def dom_at(i):
        return (i // 2) * 4 + side * 2 + i % 2

    def own_rows(i):
        return pl.ds(pl.multiple_of(i * cut, cut), cut)

    def remote(src, dst, send, recv, to):
        return pltpu.make_async_remote_copy(
            src_ref=src, dst_ref=dst, send_sem=send, recv_sem=recv, device_id=to, device_id_type=MESH
        )

    def donor_copy(k):
        to = site_of(k)
        return remote(sbuf.at[to], rbuf.at[site], d_send.at[k], d_recv.at[nsite - k], (me, dom_at(to)))

    def donor_arrival(k):
        return remote(sbuf.at[0], rbuf.at[site_of(k)], d_send.at[k], d_recv.at[k], (me, dom_at(site_of(k))))

    def partial_copy():
        return remote(psend, precv, p_send.at[0], p_recv.at[0], (me, mate))

    def forward_copy(g, k):
        v0, v1 = GROUPS[g]
        to = inst_of(k)
        return remote(
            x.at[v0:v1, own_rows(to)],
            fbuf.at[ninst - k, v0:v1],
            f_send.at[g, k],
            f_recv.at[g, ninst - k],
            (to, dom),
        )

    def forward_arrival(g, k):
        v0, v1 = GROUPS[g]
        return remote(
            x.at[v0:v1, own_rows(me)], fbuf.at[k, v0:v1], f_send.at[g, k], f_recv.at[g, k], (inst_of(k), dom)
        )

    def back_copy(g, k):
        v0, v1 = GROUPS[g]
        return remote(
            obuf.at[k, v0:v1],
            back.at[v0:v1, own_rows(me)],
            b_send.at[g, k],
            b_recv.at[g, ninst - k],
            (inst_of(k), dom),
        )

    def back_arrival(g, k):
        v0, v1 = GROUPS[g]
        return remote(
            obuf.at[k, v0:v1], back.at[v0:v1, own_rows(inst_of(k))], b_send.at[g, k], b_recv.at[g, k], (inst_of(k), dom)
        )

    def mapped_copy(k):
        to = inst_of(k)
        return remote(mbuf.at[to], mrec.at[ninst - k], m_send.at[k], m_recv.at[ninst - k], (to, dom))

    def mapped_arrival(k):
        return remote(mbuf.at[0], mrec.at[k], m_send.at[k], m_recv.at[k], (inst_of(k), dom))

    def ghost_copy(k):
        return remote(gout.at[k], gback.at[me], g_send.at[k], g_recv.at[ninst - k], (inst_of(k), dom))

    def ghost_arrival(k):
        return remote(gout.at[k], gback.at[inst_of(k)], g_send.at[k], g_recv.at[k], (inst_of(k), dom))

    def halo_copy(side):
        to = dom_of(1 if side == 0 else ndom - 1)
        return remote(hsend.at[side], hrecv.at[side], h_send.at[side], h_recv.at[side], (me, to))

    def each(count, act):
        def step(k, carry):
            act(k)
            return carry

        lax.fori_loop(1, count, step, 0)

    def peers(act):
        for k in ORDER:
            act(k)

    def sites(act):
        def step(t, carry):
            act(nsite // 2 + (1 - 2 * lax.rem(t, 2)) * ((t + 1) // 2))
            return carry

        lax.fori_loop(0, nsite - 1, step, 0)

    pairs = (
        (x_in, x),
        (part_in, part),
        (block_in, block),
        (speed_in, speed),
        (freq_in, freq),
        (time_weights_in, time_weights),
        (shift_in, shift),
        (weight_in, weight),
        (count_in, count),
    )
    arriving = [pltpu.make_async_copy(a, b, loads.at[n]) for n, (a, b) in enumerate(pairs)]
    for load in arriving:
        load.start()

    barrier = pltpu.get_barrier_semaphore()
    def greet(to):
        pl.semaphore_signal(barrier, inc=1, device_id=to, device_id_type=MESH)

    sites(lambda k: greet((me, dom_at(site_of(k)))))
    peers(lambda k: greet((inst_of(k), dom)))
    greet((me, mate))
    greet((me, dom_of(jnp.where(dom % 2 == 0, ndom - 1, 1))))

    for load in arriving:
        load.wait()
    column = send_table(part, block, dom, ndom, rows, donors)
    lane = iota(column.shape, 1).astype(jnp.float32)
    chosen = jnp.concatenate(
        [jnp.where(column == lane + float(s), 1.0, 0.0) for s in range(0, cells, 128)], axis=1
    )
    for v in range(nv):
        out = jnp.dot(chosen, x[v], precision=HIGHEST, preferred_element_type=jnp.float32)
        for i in range(nsite):
            sbuf[i, v] = out[i * 2 * cap : (i + 1) * 2 * cap]
        hsend[0, v] = x[v, cells - 1 :, :]
        hsend[1, v] = x[v, :1, :]

    pl.semaphore_wait(barrier, nsite - 1 + ninst - 1 + 2)
    halo_copy(0).start()
    halo_copy(1).start()
    sites(lambda k: donor_copy(k).start())
    for g in range(len(GROUPS)):
        peers(lambda k: forward_copy(g, k).start())

    rbuf[site] = sbuf[site]
    for v in range(nv):
        fbuf[0, v] = x[v, own_rows(me), :]

    def weights_of(target, carry):
        phase = shift[inst_of(target)]
        for k in range(ninst):
            wtab[target * ninst + k] = time_weights[jnp.bitwise_and(me + k - phase, ninst - 1)]
        return carry

    lax.fori_loop(0, ninst, weights_of, 0)
    table = jnp.concatenate(
        [weight_table(part, weight, count, whose, side, ndom, rows, donors) for whose in (dom, mate)], axis=0
    )

    halo_copy(0).wait_recv()
    halo_copy(1).wait_recv()
    edge = iota((cells, pitch), 0)
    for v in range(nv):
        u = x[v]
        low = jnp.where(dom == 0, 0.0, hrecv[0, v])
        high = jnp.where(dom == ndom - 1, 0.0, hrecv[1, v])
        below = jnp.where(edge == 0, low, pltpu.roll(u, 1, 0))
        above = jnp.where(edge == cells - 1, high, pltpu.roll(u, cells - 1, 0))
        upper = pltpu.roll(u, pitch - 1, 1)
        lower = pltpu.roll(u, 1, 1)
        base = 0.25 * (above + below + upper + lower - 4.0 * u) - speed[v] * (upper - lower) * 0.5
        res[v] = base
        res[v, :rows] = base[:rows] - 0.5 * u[:rows]

    line = spectral_line(ninst)
    half = ninst // 2
    even = [float(np.float32(0.5 * (line[j] + line[j + half]))) for j in range(half)]
    odd = [float(np.float32(0.5 * (line[j] - line[j + half]))) for j in range(half)]
    scale = -freq[0]

    def mix(g):
        v0, v1 = GROUPS[g]
        each(ninst, lambda k: forward_arrival(g, k).wait_recv())

        def tile(t, carry):
            v = v0 + t // (cut // 8)
            r = pl.multiple_of((t % (cut // 8)) * 8, 8)
            f = [fbuf[k, v, pl.ds(r, 8), :] for k in range(ninst)]
            e = [scale * (f[k] + f[k + half]) for k in range(half)]
            o = [scale * (f[k] - f[k + half]) for k in range(half)]
            for target in range(half):
                total_e = total_o = None
                for k in range(half):
                    j = target - k
                    ce = even[j % half]
                    co = odd[j] if j >= 0 else -odd[j + half]
                    total_e = ce * e[k] if total_e is None else total_e + ce * e[k]
                    total_o = co * o[k] if total_o is None else total_o + co * o[k]
                if target == 0:
                    back[v, pl.ds(pl.multiple_of(me * cut + r, 8), 8), :] = total_e + total_o
                else:
                    obuf[target, v, pl.ds(r, 8), :] = total_e + total_o
                obuf[target + half, v, pl.ds(r, 8), :] = total_e - total_o
            return carry

        lax.fori_loop(0, (v1 - v0) * (cut // 8), tile, 0)
        peers(lambda k: back_copy(g, k).start())

    def remap():
        each(nsite, lambda k: donor_arrival(k).wait_recv())
        own = []
        for v in range(nv):
            arrived = jnp.concatenate([rbuf[i, v] for i in range(nsite)], axis=0)
            both = jnp.dot(table, arrived, precision=HIGHEST, preferred_element_type=jnp.float32)
            own.append(both[:rows])
            psend[v] = both[rows:]
        partial_copy().start()
        partial_copy().wait_recv()
        for v in range(nv):
            rows_v = own[v] + precv[v]
            for s in range(ninst):
                mbuf[s, fine * v : fine * (v + 1)] = rows_v[fine * s : fine * (s + 1)]
        peers(lambda k: mapped_copy(k).start())
        mrec[0] = mbuf[me]

    def interpolate():
        each(ninst, lambda k: mapped_arrival(k).wait_recv())

        def one(target, carry):
            total = wtab[target * ninst] * mrec[0]
            for k in range(1, ninst):
                total = total + wtab[target * ninst + k] * mrec[k]
            gout[target] = total
            return carry

        lax.fori_loop(0, ninst, one, 0)
        peers(lambda k: ghost_copy(k).start())
        gback[me] = gout[0]

    mix(0)
    remap()
    mix(1)
    interpolate()
    mix(2)

    def store(v):
        return pltpu.make_async_copy(res.at[v], res_out.at[v], stores.at[v])

    each(ninst, lambda k: ghost_arrival(k).wait_recv())
    for v in range(nv):
        full = jnp.concatenate([gback[s, fine * v : fine * (v + 1)] for s in range(ninst)], axis=0)
        ghost[v] = full
        res[v, :rows] = res[v, :rows] + 0.5 * full
    store_ghost = pltpu.make_async_copy(ghost, ghost_out, stores.at[nv])
    store_ghost.start()
    for g, (v0, v1) in enumerate(GROUPS):
        each(ninst, lambda k: back_arrival(g, k).wait_recv())
        for v in range(v0, v1):
            res[v] = res[v] + back[v]
            store(v).start()

    halo_copy(0).wait_send()
    halo_copy(1).wait_send()
    each(nsite, lambda k: donor_copy(k).wait_send())
    partial_copy().wait_send()
    for g in range(len(GROUPS)):
        each(ninst, lambda k: forward_copy(g, k).wait_send())
        each(ninst, lambda k: back_copy(g, k).wait_send())
    each(ninst, lambda k: mapped_copy(k).wait_send())
    each(ninst, lambda k: ghost_copy(k).wait_send())
    for v in range(nv):
        store(v).wait()
    store_ghost.wait()


def place(res_in, ghost_in, res, ghost, held, held_ghost, loads, stores):
    count = res.shape[0]
    ways = [(res_in.at[v], held.at[v], res.at[v]) for v in range(count)]
    ways.append((ghost_in, held_ghost, ghost))
    moves = [
        (pltpu.make_async_copy(a, b, loads.at[n]), pltpu.make_async_copy(b, c, stores.at[n]))
        for n, (a, b, c) in enumerate(ways)
    ]
    for load, _ in moves:
        load.start()
    for load, store in moves:
        load.wait()
        store.start()
    for _, store in moves:
        store.wait()


def solution(mesh):
    ninst, ndom = mesh.shape["inst"], mesh.shape["dom"]

    def body(flow_state, speed, freq, time_weights, shift, part, block, count, weight):
        x = flow_state[0]
        nv, cells, pitch = x.shape
        rows = part.shape[0] // ndom
        donors = part.shape[1]
        cap = rows * donors // ndom
        cut = cells // ninst
        fine = rows // ninst
        groups = len(GROUPS)
        hbm = pl.BlockSpec(memory_space=pltpu.HBM)
        f32 = jnp.float32
        dma = pltpu.SemaphoreType.DMA
        res, ghost = pl.pallas_call(
            functools.partial(kernel, ninst, ndom),
            out_shape=(
                jax.ShapeDtypeStruct((nv, cells, pitch), f32),
                jax.ShapeDtypeStruct((nv, rows, pitch), f32),
            ),
            in_specs=[hbm] * 9,
            out_specs=(hbm, hbm),
            scratch_shapes=[
                pltpu.VMEM(x.shape, f32),
                pltpu.SMEM(speed.shape, f32),
                pltpu.SMEM(freq.shape, f32),
                pltpu.SMEM(time_weights.shape, f32),
                pltpu.SMEM(shift.shape, jnp.int32),
                pltpu.VMEM(part.T.shape, jnp.int32),
                pltpu.VMEM(part.T.shape, jnp.int32),
                pltpu.VMEM(part.T.shape, f32),
                pltpu.VMEM((1, count.shape[0]), jnp.int32),
                dma((9,)),
                pltpu.VMEM((nv, cells, pitch), f32),
                pltpu.VMEM((nv, rows, pitch), f32),
                dma((nv + 1,)),
                pltpu.VMEM((ndom // 2, nv, 2 * cap, pitch), f32),
                pltpu.VMEM((ndom // 2, nv, 2 * cap, pitch), f32),
                pltpu.VMEM((ninst, nv, cut, pitch), f32),
                pltpu.VMEM((ninst, nv, cut, pitch), f32),
                pltpu.VMEM((nv, cells, pitch), f32),
                pltpu.VMEM((nv, rows, pitch), f32),
                pltpu.VMEM((nv, rows, pitch), f32),
                pltpu.VMEM((ninst, nv * fine, pitch), f32),
                pltpu.VMEM((ninst, nv * fine, pitch), f32),
                pltpu.VMEM((ninst, nv * fine, pitch), f32),
                pltpu.VMEM((ninst, nv * fine, pitch), f32),
                pltpu.VMEM((2, nv, 1, pitch), f32),
                pltpu.VMEM((2, nv, 1, pitch), f32),
                pltpu.SMEM((ninst * ninst,), f32),
                dma((ndom // 2,)),
                dma((ndom // 2,)),
                dma((groups, ninst)),
                dma((groups, ninst)),
                dma((groups, ninst)),
                dma((groups, ninst)),
                dma((1,)),
                dma((1,)),
                dma((ninst,)),
                dma((ninst,)),
                dma((ninst,)),
                dma((ninst,)),
                dma((2,)),
                dma((2,)),
            ],
            compiler_params=pltpu.CompilerParams(
                collective_id=0, has_side_effects=True, vmem_limit_bytes=VMEM
            ),
            name="harmonic_residual",
        )(x, speed, freq, time_weights, shift, part.T, block.T, weight.T, count[None])
        res, ghost = pl.pallas_call(
            place,
            out_shape=(
                jax.ShapeDtypeStruct((nv, cells, pitch), f32),
                jax.ShapeDtypeStruct((nv, rows, pitch), f32),
            ),
            in_specs=[hbm, hbm],
            out_specs=(hbm, hbm),
            scratch_shapes=[
                pltpu.VMEM((nv, cells, pitch), f32),
                pltpu.VMEM((nv, rows, pitch), f32),
                dma((nv + 1,)),
                dma((nv + 1,)),
            ],
            compiler_params=pltpu.CompilerParams(vmem_limit_bytes=VMEM),
            name="place_results",
        )(res, ghost)
        return res[None], ghost[None]

    in_specs = (P("inst", None, "dom", None), P(), P(), P(), P(), P(), P(), P(), P())
    out_specs = (P("inst", None, "dom", None), P("inst", None, "dom", None))
    return jax.shard_map(body, mesh=mesh, in_specs=in_specs, out_specs=out_specs, check_vma=False)
```

```python
import functools

import jax
import jax.numpy as jnp
import numpy as np
from jax import lax
from jax.experimental import pallas as pl
from jax.experimental.pallas import tpu as pltpu
from jax.sharding import PartitionSpec as P

HIGHEST = lax.Precision.HIGHEST
VMEM = 32 << 20
MESH = pl.DeviceIdType.MESH
GROUPS = ((0, 5),)
ORDER = (2, 10, 6, 14, 9, 5, 11, 7, 1, 13, 3, 15, 8, 4, 12)


def spectral_line(length):
    j = np.arange(length)
    safe = np.where(j == 0, 1, j)
    line = 0.5 * np.where(j % 2 == 0, 1.0, -1.0) / np.tan(np.pi * safe / length)
    return np.where(j == 0, -2.0, line) + 2.0 / length


def iota(shape, dim):
    return lax.broadcasted_iota(jnp.int32, shape, dim)


def send_table(part_ref, block_ref, dom, ndom, rows, donors):
    lanes = 128
    chunks = ndom * rows // lanes
    parts = jnp.concatenate([part_ref[:, lanes * g : lanes * (g + 1)] for g in range(chunks)], axis=0)
    blocks = jnp.concatenate([block_ref[:, lanes * g : lanes * (g + 1)] for g in range(chunks)], axis=0)
    count = chunks * donors
    cap = rows * donors // ndom
    per = lanes // rows
    wanted = parts == dom
    ones = jnp.where(wanted, 1.0, 0.0)
    a, b = iota((lanes, lanes), 0), iota((lanes, lanes), 1)
    same = (a // rows) == (b // rows)
    before = jnp.where(same & (a < b), 1.0, 0.0)
    whole = jnp.where(same, 1.0, 0.0)
    ra, rb = iota((count, count), 0), iota((count, count), 1)
    lower = jnp.where(((ra // donors) == (rb // donors)) & (rb < ra), 1.0, 0.0)
    dot = functools.partial(jnp.dot, preferred_element_type=jnp.float32)
    rank = dot(ones, before) + dot(lower, dot(ones, whole))
    total = jnp.zeros((count, lanes), jnp.float32)
    values = blocks.astype(jnp.float32)
    for c in range(cap):
        picked = jnp.where(wanted & (rank == float(c)), values, 0.0)
        group = a // rows
        spread = jnp.where((b % (per * cap)) == ((group % 2) * 2 + group // 2) * cap + c, 1.0, 0.0)
        total = total + dot(picked, spread)
    row, lane = iota((count, lanes), 0), iota((count, lanes), 1)
    line = jnp.sum(
        jnp.where((lane // (per * cap)) == (row // donors), total, 0.0), axis=0, keepdims=True
    )
    return jnp.transpose(jnp.broadcast_to(line, (lanes, lanes)))


def weight_table(part_ref, weight_ref, count_ref, dom, side, ndom, rows, donors):
    lanes = 128
    per = lanes // rows
    cap = rows * donors // ndom
    at = pl.ds(pl.multiple_of((dom // per) * lanes, lanes), lanes)
    own = jnp.concatenate(
        [
            part_ref[:, at].astype(jnp.float32),
            weight_ref[:, at],
            jnp.broadcast_to(count_ref[:, at].astype(jnp.float32), (8, lanes)),
        ],
        axis=0,
    )
    a, b = iota((lanes, lanes), 0), iota((lanes, lanes), 1)
    pick = jnp.where(a == (dom % per) * rows + b % rows, 1.0, 0.0)
    own = jnp.dot(own, pick, precision=HIGHEST, preferred_element_type=jnp.float32)
    row, lane = iota((donors, lanes), 0), iota((donors, lanes), 1)
    mine = (lane // rows) == row
    part = jnp.sum(jnp.where(mine, own[:donors], 0.0), axis=0, keepdims=True)
    live = mine & (row.astype(jnp.float32) < own[2 * donors : 3 * donors])
    weight = jnp.sum(jnp.where(live, own[donors : 2 * donors], 0.0), axis=0, keepdims=True)
    part_row = jnp.broadcast_to(part, (lanes, lanes))
    part_col = jnp.transpose(part_row)
    rank = jnp.sum(jnp.where((part_row == part_col) & (a < b), 1.0, 0.0), axis=0, keepdims=True)
    named = part.astype(jnp.int32)
    site = (named // 4) * 2 + named % 2
    slot = (site * 2 + (dom // 2) % 2).astype(jnp.float32) * cap + rank
    slot = jnp.where((named // 2) % 2 == side, slot, -1.0)
    slot_col = jnp.transpose(jnp.broadcast_to(slot, (lanes, lanes)))
    weight_col = jnp.transpose(jnp.broadcast_to(weight, (lanes, lanes)))
    spread = jnp.where(slot_col == b.astype(jnp.float32), weight_col, 0.0)
    top = sum(spread[rows * k : rows * (k + 1)] for k in range(donors))
    bottom = sum(weight_col[rows * k : rows * (k + 1)] for k in range(donors))
    return top / bottom


def kernel(
    ninst,
    ndom,
    x_in,
    speed_in,
    freq_in,
    time_weights_in,
    shift_in,
    part_in,
    block_in,
    weight_in,
    count_in,
    res,
    ghost,
    x,
    speed,
    freq,
    time_weights,
    shift,
    part,
    block,
    weight,
    count,
    loads,
    sbuf,
    rbuf,
    fbuf,
    obuf,
    back,
    psend,
    precv,
    mbuf,
    mrec,
    gout,
    gback,
    hsend,
    hrecv,
    wtab,
    go,
    d_send,
    d_recv,
    f_send,
    f_recv,
    b_send,
    b_recv,
    p_send,
    p_recv,
    m_send,
    m_recv,
    g_send,
    g_recv,
    h_send,
    h_recv,
):
    nv, cells, pitch = x.shape
    rows = ghost.shape[1]
    donors = part.shape[0]
    cap = rows * donors // ndom
    cut = cells // ninst
    fine = rows // ninst
    me, dom = lax.axis_index("inst"), lax.axis_index("dom")

    def inst_of(k):
        return lax.rem(me + k, ninst)

    def dom_of(k):
        return lax.rem(dom + k, ndom)

    nsite = ndom // 2
    side = (dom // 2) % 2
    site = (dom // 4) * 2 + dom % 2
    mate = dom + 2 - 4 * side
    core = dom % 2
    depth = ndom // 4
    layer = dom // 4

    def second_core_at(z, s):
        return (me, lax.rem(z + depth, depth) * 4 + s * 2 + 1)

    def site_of(k):
        return lax.rem(site + k, nsite)

    def dom_at(i):
        return (i // 2) * 4 + side * 2 + i % 2

    def own_rows(i):
        return pl.ds(pl.multiple_of(i * cut, cut), cut)

    def remote(src, dst, send, recv, to):
        return pltpu.make_async_remote_copy(
            src_ref=src, dst_ref=dst, send_sem=send, recv_sem=recv, device_id=to, device_id_type=MESH
        )

    def donor_copy(k):
        to = site_of(k)
        return remote(sbuf.at[to], rbuf.at[site], d_send.at[k], d_recv.at[nsite - k], (me, dom_at(to)))

    def donor_arrival(k):
        return remote(sbuf.at[0], rbuf.at[site_of(k)], d_send.at[k], d_recv.at[k], (me, dom_at(site_of(k))))

    def partial_copy():
        return remote(psend, precv, p_send.at[0], p_recv.at[0], (me, mate))

    def forward_copy(g, k):
        v0, v1 = GROUPS[g]
        to = inst_of(k)
        return remote(
            x.at[v0:v1, own_rows(to)],
            fbuf.at[ninst - k, v0:v1],
            f_send.at[g, k],
            f_recv.at[g, ninst - k],
            (to, dom),
        )

    def forward_arrival(g, k):
        v0, v1 = GROUPS[g]
        return remote(
            x.at[v0:v1, own_rows(me)], fbuf.at[k, v0:v1], f_send.at[g, k], f_recv.at[g, k], (inst_of(k), dom)
        )

    def back_copy(g, k):
        v0, v1 = GROUPS[g]
        return remote(
            obuf.at[k, v0:v1],
            back.at[v0:v1, own_rows(me)],
            b_send.at[g, k],
            b_recv.at[g, ninst - k],
            (inst_of(k), dom),
        )

    def back_arrival(g, k):
        v0, v1 = GROUPS[g]
        return remote(
            obuf.at[k, v0:v1], back.at[v0:v1, own_rows(inst_of(k))], b_send.at[g, k], b_recv.at[g, k], (inst_of(k), dom)
        )

    def mapped_copy(k):
        to = inst_of(k)
        return remote(mbuf.at[to], mrec.at[ninst - k], m_send.at[k], m_recv.at[ninst - k], (to, dom))

    def mapped_arrival(k):
        return remote(mbuf.at[0], mrec.at[k], m_send.at[k], m_recv.at[k], (inst_of(k), dom))

    def ghost_copy(k):
        return remote(gout.at[k], gback.at[me], g_send.at[k], g_recv.at[ninst - k], (inst_of(k), dom))

    def ghost_arrival(k):
        return remote(gout.at[k], gback.at[inst_of(k)], g_send.at[k], g_recv.at[k], (inst_of(k), dom))

    def halo_copy(side):
        to = dom_of(1 if side == 0 else ndom - 1)
        return remote(hsend.at[side], hrecv.at[side], h_send.at[side], h_recv.at[side], (me, to))

    def each(count, act):
        def step(k, carry):
            act(k)
            return carry

        lax.fori_loop(1, count, step, 0)

    def peers(act):
        for k in ORDER:
            act(k)

    def sites(act):
        def step(t, carry):
            act(nsite // 2 + (1 - 2 * lax.rem(t, 2)) * ((t + 1) // 2))
            return carry

        lax.fori_loop(0, nsite - 1, step, 0)

    pairs = (
        (x_in, x),
        (part_in, part),
        (block_in, block),
        (speed_in, speed),
        (freq_in, freq),
        (time_weights_in, time_weights),
        (shift_in, shift),
        (weight_in, weight),
        (count_in, count),
    )
    arriving = [pltpu.make_async_copy(a, b, loads.at[n]) for n, (a, b) in enumerate(pairs)]
    for load in arriving:
        load.start()

    barrier = pltpu.get_barrier_semaphore()

    def greet(to):
        pl.semaphore_signal(barrier, inc=1, device_id=to, device_id_type=MESH)

    peers(lambda k: greet((inst_of(k), dom - core)))
    greet((me, dom + 1 - 2 * core))
    for k in range(1, depth):
        greet(second_core_at(layer + k, side))
    greet(second_core_at(layer, 1 - side))
    greet(second_core_at(layer - 1 + 2 * side, 1 - side))

    for load in arriving:
        load.wait()
    column = send_table(part, block, dom, ndom, rows, donors)
    lane = iota(column.shape, 1).astype(jnp.float32)
    chosen = jnp.concatenate(
        [jnp.where(column == lane + float(s), 1.0, 0.0) for s in range(0, cells, 128)], axis=1
    )
    for v in range(nv):
        out = jnp.dot(chosen, x[v], precision=HIGHEST, preferred_element_type=jnp.float32)
        for i in range(nsite):
            sbuf[i, v] = out[i * 2 * cap : (i + 1) * 2 * cap]
        hsend[0, v] = x[v, cells - 1 :, :]
        hsend[1, v] = x[v, :1, :]

    @pl.when(core == 0)
    def _():
        pl.semaphore_wait(barrier, 2 * (ninst - 1) + 1)
        pl.semaphore_signal(go.at[0], inc=1, device_id=(me, dom + 1), device_id_type=MESH)

    @pl.when(core == 1)
    def _():
        pl.semaphore_wait(go.at[0], 1)

    for g in range(len(GROUPS)):
        peers(lambda k: forward_copy(g, k).start())

    @pl.when(core == 1)
    def _():
        pl.semaphore_wait(barrier, 2 * (depth - 1) + 2 + 2 + 1)
        pl.semaphore_signal(go.at[1], inc=1, device_id=(me, dom - 1), device_id_type=MESH)

    @pl.when(core == 0)
    def _():
        pl.semaphore_wait(go.at[1], 1)

    sites(lambda k: donor_copy(k).start())
    halo_copy(0).start()
    halo_copy(1).start()

    rbuf[site] = sbuf[site]
    for v in range(nv):
        fbuf[0, v] = x[v, own_rows(me), :]

    def weights_of(target, carry):
        phase = shift[inst_of(target)]
        for k in range(ninst):
            wtab[target * ninst + k] = time_weights[jnp.bitwise_and(me + k - phase, ninst - 1)]
        return carry

    lax.fori_loop(0, ninst, weights_of, 0)
    table = jnp.concatenate(
        [weight_table(part, weight, count, whose, side, ndom, rows, donors) for whose in (dom, mate)], axis=0
    )

    edge = iota((cells, pitch), 0)
    for v in range(nv):
        u = x[v]
        below = jnp.where(edge == 0, 0.0, pltpu.roll(u, 1, 0))
        above = jnp.where(edge == cells - 1, 0.0, pltpu.roll(u, cells - 1, 0))
        upper = pltpu.roll(u, pitch - 1, 1)
        lower = pltpu.roll(u, 1, 1)
        base = 0.25 * (above + below + upper + lower - 4.0 * u) - speed[v] * (upper - lower) * 0.5
        res[v] = base
        res[v, :rows] = base[:rows] - 0.5 * u[:rows]

    line = spectral_line(ninst)
    half = ninst // 2
    even = [float(np.float32(0.5 * (line[j] + line[j + half]))) for j in range(half)]
    odd = [float(np.float32(0.5 * (line[j] - line[j + half]))) for j in range(half)]
    scale = -freq[0]

    def mix(g):
        v0, v1 = GROUPS[g]
        each(ninst, lambda k: forward_arrival(g, k).wait_recv())

        def tile(t, carry):
            v = v0 + t // (cut // 8)
            r = pl.multiple_of((t % (cut // 8)) * 8, 8)
            f = [fbuf[k, v, pl.ds(r, 8), :] for k in range(ninst)]
            e = [scale * (f[k] + f[k + half]) for k in range(half)]
            o = [scale * (f[k] - f[k + half]) for k in range(half)]
            for target in range(half):
                total_e = total_o = None
                for k in range(half):
                    j = target - k
                    ce = even[j % half]
                    co = odd[j] if j >= 0 else -odd[j + half]
                    total_e = ce * e[k] if total_e is None else total_e + ce * e[k]
                    total_o = co * o[k] if total_o is None else total_o + co * o[k]
                if target == 0:
                    back[v, pl.ds(pl.multiple_of(me * cut + r, 8), 8), :] = total_e + total_o
                else:
                    obuf[target, v, pl.ds(r, 8), :] = total_e + total_o
                obuf[target + half, v, pl.ds(r, 8), :] = total_e - total_o
            return carry

        lax.fori_loop(0, (v1 - v0) * (cut // 8), tile, 0)
        peers(lambda k: back_copy(g, k).start())

    def remap():
        each(nsite, lambda k: donor_arrival(k).wait_recv())
        own = []
        for v in range(nv):
            arrived = jnp.concatenate([rbuf[i, v] for i in range(nsite)], axis=0)
            both = jnp.dot(table, arrived, precision=HIGHEST, preferred_element_type=jnp.float32)
            own.append(both[:rows])
            psend[v] = both[rows:]
        partial_copy().start()
        partial_copy().wait_recv()
        for v in range(nv):
            rows_v = own[v] + precv[v]
            for s in range(ninst):
                mbuf[s, fine * v : fine * (v + 1)] = rows_v[fine * s : fine * (s + 1)]
        peers(lambda k: mapped_copy(k).start())
        mrec[0] = mbuf[me]

    def interpolate():
        each(ninst, lambda k: mapped_arrival(k).wait_recv())

        def one(target, carry):
            total = wtab[target * ninst] * mrec[0]
            for k in range(1, ninst):
                total = total + wtab[target * ninst + k] * mrec[k]
            gout[target] = total
            return carry

        lax.fori_loop(0, ninst, one, 0)
        peers(lambda k: ghost_copy(k).start())
        gback[me] = gout[0]

    remap()
    mix(0)
    interpolate()

    halo_copy(0).wait_recv()
    halo_copy(1).wait_recv()
    for v in range(nv):
        res[v, :1] = res[v, :1] + jnp.where(dom == 0, 0.0, 0.25 * hrecv[0, v])
        res[v, cells - 1 :] = res[v, cells - 1 :] + jnp.where(dom == ndom - 1, 0.0, 0.25 * hrecv[1, v])
    each(ninst, lambda k: ghost_arrival(k).wait_recv())
    for v in range(nv):
        full = jnp.concatenate([gback[s, fine * v : fine * (v + 1)] for s in range(ninst)], axis=0)
        ghost[v] = full
        res[v, :rows] = res[v, :rows] + 0.5 * full
    for g, (v0, v1) in enumerate(GROUPS):
        each(ninst, lambda k: back_arrival(g, k).wait_recv())
        for v in range(v0, v1):
            res[v] = res[v] + back[v]

    halo_copy(0).wait_send()
    halo_copy(1).wait_send()
    each(nsite, lambda k: donor_copy(k).wait_send())
    partial_copy().wait_send()
    for g in range(len(GROUPS)):
        each(ninst, lambda k: forward_copy(g, k).wait_send())
        each(ninst, lambda k: back_copy(g, k).wait_send())
    each(ninst, lambda k: mapped_copy(k).wait_send())
    each(ninst, lambda k: ghost_copy(k).wait_send())


def place(res_in, ghost_in, res, ghost, sems):
    moves = [
        pltpu.make_async_copy(res_in, res, sems.at[0]),
        pltpu.make_async_copy(ghost_in, ghost, sems.at[1]),
    ]
    for move in moves:
        move.start()
    for move in moves:
        move.wait()


def solution(mesh):
    ninst, ndom = mesh.shape["inst"], mesh.shape["dom"]

    def body(flow_state, speed, freq, time_weights, shift, part, block, count, weight):
        x = flow_state[0]
        nv, cells, pitch = x.shape
        rows = part.shape[0] // ndom
        donors = part.shape[1]
        cap = rows * donors // ndom
        cut = cells // ninst
        fine = rows // ninst
        groups = len(GROUPS)
        hbm = pl.BlockSpec(memory_space=pltpu.HBM)
        vmem = pl.BlockSpec(memory_space=pltpu.VMEM)
        f32 = jnp.float32
        dma = pltpu.SemaphoreType.DMA
        given = (x, speed, freq, time_weights, shift, part.T, block.T, weight.T, count[None])
        given = [a if a.size == 1 else pltpu.with_memory_space_constraint(a, pltpu.HBM) for a in given]
        res, ghost = pl.pallas_call(
            functools.partial(kernel, ninst, ndom),
            out_shape=(pltpu.VMEM((nv, cells, pitch), f32), pltpu.VMEM((nv, rows, pitch), f32)),
            in_specs=[hbm] * 9,
            out_specs=(vmem, vmem),
            scratch_shapes=[
                pltpu.VMEM(x.shape, f32),
                pltpu.SMEM(speed.shape, f32),
                pltpu.SMEM(freq.shape, f32),
                pltpu.SMEM(time_weights.shape, f32),
                pltpu.SMEM(shift.shape, jnp.int32),
                pltpu.VMEM(part.T.shape, jnp.int32),
                pltpu.VMEM(part.T.shape, jnp.int32),
                pltpu.VMEM(part.T.shape, f32),
                pltpu.VMEM((1, count.shape[0]), jnp.int32),
                dma((9,)),
                pltpu.VMEM((ndom // 2, nv, 2 * cap, pitch), f32),
                pltpu.VMEM((ndom // 2, nv, 2 * cap, pitch), f32),
                pltpu.VMEM((ninst, nv, cut, pitch), f32),
                pltpu.VMEM((ninst, nv, cut, pitch), f32),
                pltpu.VMEM((nv, cells, pitch), f32),
                pltpu.VMEM((nv, rows, pitch), f32),
                pltpu.VMEM((nv, rows, pitch), f32),
                pltpu.VMEM((ninst, nv * fine, pitch), f32),
                pltpu.VMEM((ninst, nv * fine, pitch), f32),
                pltpu.VMEM((ninst, nv * fine, pitch), f32),
                pltpu.VMEM((ninst, nv * fine, pitch), f32),
                pltpu.VMEM((2, nv, 1, pitch), f32),
                pltpu.VMEM((2, nv, 1, pitch), f32),
                pltpu.SMEM((ninst * ninst,), f32),
                pltpu.SemaphoreType.REGULAR((2,)),
                dma((ndom // 2,)),
                dma((ndom // 2,)),
                dma((groups, ninst)),
                dma((groups, ninst)),
                dma((groups, ninst)),
                dma((groups, ninst)),
                dma((1,)),
                dma((1,)),
                dma((ninst,)),
                dma((ninst,)),
                dma((ninst,)),
                dma((ninst,)),
                dma((2,)),
                dma((2,)),
            ],
            compiler_params=pltpu.CompilerParams(
                collective_id=0, has_side_effects=True, vmem_limit_bytes=VMEM
            ),
            name="harmonic_residual",
        )(*given)
        res, ghost = pl.pallas_call(
            place,
            out_shape=(
                jax.ShapeDtypeStruct((nv, cells, pitch), f32),
                jax.ShapeDtypeStruct((nv, rows, pitch), f32),
            ),
            in_specs=[vmem, vmem],
            out_specs=(hbm, hbm),
            scratch_shapes=[dma((2,))],
            name="place_results",
        )(*(pltpu.with_memory_space_constraint(a, pltpu.VMEM) for a in (res, ghost)))
        return res[None], ghost[None]

    in_specs = (P("inst", None, "dom", None), P(), P(), P(), P(), P(), P(), P(), P())
    out_specs = (P("inst", None, "dom", None), P("inst", None, "dom", None))
    return jax.shard_map(body, mesh=mesh, in_specs=in_specs, out_specs=out_specs, check_vma=False)
```

```python
import functools

import jax
import jax.numpy as jnp
import numpy as np
from jax import lax
from jax.experimental import pallas as pl
from jax.experimental.pallas import tpu as pltpu
from jax.sharding import PartitionSpec as P

HIGHEST = lax.Precision.HIGHEST
VMEM = 32 << 20
MESH = pl.DeviceIdType.MESH
GROUPS = ((0, 5),)
ORDER = (12, 4, 8, 15, 3, 13, 1, 7, 11, 5, 9, 14, 6, 10, 2)


def spectral_line(length):
    j = np.arange(length)
    safe = np.where(j == 0, 1, j)
    line = 0.5 * np.where(j % 2 == 0, 1.0, -1.0) / np.tan(np.pi * safe / length)
    return np.where(j == 0, -2.0, line) + 2.0 / length


def iota(shape, dim):
    return lax.broadcasted_iota(jnp.int32, shape, dim)


def send_table(part_ref, block_ref, dom, ndom, rows, donors):
    lanes = 128
    chunks = ndom * rows // lanes
    parts = jnp.concatenate([part_ref[:, lanes * g : lanes * (g + 1)] for g in range(chunks)], axis=0)
    blocks = jnp.concatenate([block_ref[:, lanes * g : lanes * (g + 1)] for g in range(chunks)], axis=0)
    count = chunks * donors
    cap = rows * donors // ndom
    per = lanes // rows
    wanted = parts == dom
    ones = jnp.where(wanted, 1.0, 0.0)
    a, b = iota((lanes, lanes), 0), iota((lanes, lanes), 1)
    same = (a // rows) == (b // rows)
    before = jnp.where(same & (a < b), 1.0, 0.0)
    whole = jnp.where(same, 1.0, 0.0)
    ra, rb = iota((count, count), 0), iota((count, count), 1)
    lower = jnp.where(((ra // donors) == (rb // donors)) & (rb < ra), 1.0, 0.0)
    dot = functools.partial(jnp.dot, preferred_element_type=jnp.float32)
    rank = dot(ones, before) + dot(lower, dot(ones, whole))
    total = jnp.zeros((count, lanes), jnp.float32)
    values = blocks.astype(jnp.float32)
    for c in range(cap):
        picked = jnp.where(wanted & (rank == float(c)), values, 0.0)
        group = a // rows
        spread = jnp.where((b % (per * cap)) == ((group % 2) * 2 + group // 2) * cap + c, 1.0, 0.0)
        total = total + dot(picked, spread)
    row, lane = iota((count, lanes), 0), iota((count, lanes), 1)
    line = jnp.sum(
        jnp.where((lane // (per * cap)) == (row // donors), total, 0.0), axis=0, keepdims=True
    )
    return jnp.transpose(jnp.broadcast_to(line, (lanes, lanes)))


def weight_table(part_ref, weight_ref, count_ref, dom, side, ndom, rows, donors):
    lanes = 128
    per = lanes // rows
    cap = rows * donors // ndom
    at = pl.ds(pl.multiple_of((dom // per) * lanes, lanes), lanes)
    own = jnp.concatenate(
        [
            part_ref[:, at].astype(jnp.float32),
            weight_ref[:, at],
            jnp.broadcast_to(count_ref[:, at].astype(jnp.float32), (8, lanes)),
        ],
        axis=0,
    )
    a, b = iota((lanes, lanes), 0), iota((lanes, lanes), 1)
    pick = jnp.where(a == (dom % per) * rows + b % rows, 1.0, 0.0)
    own = jnp.dot(own, pick, precision=HIGHEST, preferred_element_type=jnp.float32)
    row, lane = iota((donors, lanes), 0), iota((donors, lanes), 1)
    mine = (lane // rows) == row
    part = jnp.sum(jnp.where(mine, own[:donors], 0.0), axis=0, keepdims=True)
    live = mine & (row.astype(jnp.float32) < own[2 * donors : 3 * donors])
    weight = jnp.sum(jnp.where(live, own[donors : 2 * donors], 0.0), axis=0, keepdims=True)
    part_row = jnp.broadcast_to(part, (lanes, lanes))
    part_col = jnp.transpose(part_row)
    rank = jnp.sum(jnp.where((part_row == part_col) & (a < b), 1.0, 0.0), axis=0, keepdims=True)
    named = part.astype(jnp.int32)
    site = (named // 4) * 2 + named % 2
    slot = (site * 2 + (dom // 2) % 2).astype(jnp.float32) * cap + rank
    slot = jnp.where((named // 2) % 2 == side, slot, -1.0)
    slot_col = jnp.transpose(jnp.broadcast_to(slot, (lanes, lanes)))
    weight_col = jnp.transpose(jnp.broadcast_to(weight, (lanes, lanes)))
    spread = jnp.where(slot_col == b.astype(jnp.float32), weight_col, 0.0)
    top = sum(spread[rows * k : rows * (k + 1)] for k in range(donors))
    bottom = sum(weight_col[rows * k : rows * (k + 1)] for k in range(donors))
    return top / bottom


def kernel(
    ninst,
    ndom,
    x_in,
    speed_in,
    freq_in,
    time_weights_in,
    shift_in,
    part_in,
    block_in,
    weight_in,
    count_in,
    res,
    ghost,
    x,
    speed,
    freq,
    time_weights,
    shift,
    part,
    block,
    weight,
    count,
    loads,
    sbuf,
    rbuf,
    fbuf,
    obuf,
    back,
    mbuf,
    mrec,
    gout,
    gback,
    hsend,
    hrecv,
    wtab,
    go,
    d_send,
    d_recv,
    f_send,
    f_recv,
    b_send,
    b_recv,
    m_send,
    m_recv,
    g_send,
    g_recv,
    h_send,
    h_recv,
):
    nv, cells, pitch = x.shape
    rows = ghost.shape[1]
    donors = part.shape[0]
    cap = rows * donors // ndom
    cut = cells // ninst
    fine = rows // ninst
    me, dom = lax.axis_index("inst"), lax.axis_index("dom")

    def inst_of(k):
        return lax.rem(me + k, ninst)

    def dom_of(k):
        return lax.rem(dom + k, ndom)

    nsite = ndom // 2
    side = (dom // 2) % 2
    site = (dom // 4) * 2 + dom % 2
    mate = dom + 2 - 4 * side
    core = dom % 2
    depth = ndom // 4
    layer = dom // 4

    def first_core_at(z, s):
        return lax.rem(z + depth, depth) * 4 + s * 2

    def site_of(k):
        return lax.rem(site + k, nsite)

    def dom_at(i):
        return (i // 2) * 4 + side * 2 + i % 2

    def own_rows(i):
        return pl.ds(pl.multiple_of(i * cut, cut), cut)

    def remote(src, dst, send, recv, to):
        return pltpu.make_async_remote_copy(
            src_ref=src, dst_ref=dst, send_sem=send, recv_sem=recv, device_id=to, device_id_type=MESH
        )

    def donor_copy(k):
        to = site_of(k)
        return remote(sbuf.at[to], rbuf.at[site], d_send.at[k], d_recv.at[nsite - k], (me, dom_at(to)))

    def donor_arrival(k):
        return remote(sbuf.at[0], rbuf.at[site_of(k)], d_send.at[k], d_recv.at[k], (me, dom_at(site_of(k))))

    def forward_copy(g, k):
        v0, v1 = GROUPS[g]
        to = inst_of(k)
        return remote(
            x.at[v0:v1, own_rows(to)],
            fbuf.at[ninst - k, v0:v1],
            f_send.at[g, k],
            f_recv.at[g, ninst - k],
            (to, dom),
        )

    def forward_arrival(g, k):
        v0, v1 = GROUPS[g]
        return remote(
            x.at[v0:v1, own_rows(me)], fbuf.at[k, v0:v1], f_send.at[g, k], f_recv.at[g, k], (inst_of(k), dom)
        )

    def back_copy(g, k):
        v0, v1 = GROUPS[g]
        return remote(
            obuf.at[k, v0:v1],
            back.at[v0:v1, own_rows(me)],
            b_send.at[g, k],
            b_recv.at[g, ninst - k],
            (inst_of(k), dom),
        )

    def back_arrival(g, k):
        v0, v1 = GROUPS[g]
        return remote(
            obuf.at[k, v0:v1], back.at[v0:v1, own_rows(inst_of(k))], b_send.at[g, k], b_recv.at[g, k], (inst_of(k), dom)
        )

    def mapped_copy(n, k):
        to, slot = inst_of(k), (ninst - k) % ninst
        return remote(
            mbuf.at[n, to], mrec.at[n, slot], m_send.at[n, k], m_recv.at[n, slot], (to, mate if n else dom)
        )

    def mapped_arrival(n, k):
        return remote(
            mbuf.at[n, 0], mrec.at[n, k], m_send.at[n, k], m_recv.at[n, k], (inst_of(k), mate if n else dom)
        )

    def ghost_copy(k):
        return remote(gout.at[k], gback.at[me], g_send.at[k], g_recv.at[ninst - k], (inst_of(k), dom))

    def ghost_arrival(k):
        return remote(gout.at[k], gback.at[inst_of(k)], g_send.at[k], g_recv.at[k], (inst_of(k), dom))

    def halo_copy(side):
        to = dom_of(1 if side == 0 else ndom - 1)
        return remote(hsend.at[side], hrecv.at[side], h_send.at[side], h_recv.at[side], (me, to))

    def each(count, act):
        def step(k, carry):
            act(k)
            return carry

        lax.fori_loop(1, count, step, 0)

    def peers(act):
        for k in ORDER:
            act(k)

    def sites(act):
        def step(t, carry):
            act(nsite // 2 + (1 - 2 * lax.rem(t, 2)) * ((t + 1) // 2))
            return carry

        lax.fori_loop(0, nsite - 1, step, 0)

    barrier = pltpu.get_barrier_semaphore()

    def greet(to):
        pl.semaphore_signal(barrier, inc=1, device_id=to, device_id_type=MESH)

    peers(lambda k: greet((inst_of(k), dom)))

    @pl.when(core == 1)
    def _():
        greet((me, dom - 1))

    for k in range(1, depth):
        greet((me, first_core_at(layer + k, side)))
    greet((me, first_core_at(layer - 1 + 2 * side, 1 - side)))
    for k in (0, *ORDER):
        greet((inst_of(k), first_core_at(layer, 1 - side)))

    pairs = (
        (x_in, x),
        (part_in, part),
        (block_in, block),
        (speed_in, speed),
        (freq_in, freq),
        (time_weights_in, time_weights),
        (shift_in, shift),
        (weight_in, weight),
        (count_in, count),
    )
    arriving = [pltpu.make_async_copy(a, b, loads.at[n]) for n, (a, b) in enumerate(pairs)]
    for load in arriving:
        load.start()

    for load in arriving:
        load.wait()
    column = send_table(part, block, dom, ndom, rows, donors)
    lane = iota(column.shape, 1).astype(jnp.float32)
    chosen = jnp.concatenate(
        [jnp.where(column == lane + float(s), 1.0, 0.0) for s in range(0, cells, 128)], axis=1
    )
    for v in range(nv):
        out = jnp.dot(chosen, x[v], precision=HIGHEST, preferred_element_type=jnp.float32)
        for i in range(nsite):
            sbuf[i, v] = out[i * 2 * cap : (i + 1) * 2 * cap]
        hsend[0, v] = x[v, cells - 1 :, :]
        hsend[1, v] = x[v, :1, :]

    @pl.when(core == 1)
    def _():
        pl.semaphore_wait(barrier, ninst - 1)

    @pl.when(core == 0)
    def _():
        pl.semaphore_wait(barrier, ninst - 1 + 1 + 2 * (depth - 1) + 2 + 2 * ninst)
        pl.semaphore_signal(go.at[0], inc=1, device_id=(me, dom + 1), device_id_type=MESH)

    for g in range(len(GROUPS)):
        peers(lambda k: forward_copy(g, k).start())

    @pl.when(core == 1)
    def _():
        pl.semaphore_wait(go.at[0], 1)

    sites(lambda k: donor_copy(k).start())
    halo_copy(0).start()
    halo_copy(1).start()

    rbuf[site] = sbuf[site]
    for v in range(nv):
        fbuf[0, v] = x[v, own_rows(me), :]

    def weights_of(target, carry):
        phase = shift[inst_of(target)]
        for k in range(ninst):
            wtab[target * ninst + k] = time_weights[jnp.bitwise_and(me + k - phase, ninst - 1)]
        return carry

    lax.fori_loop(0, ninst, weights_of, 0)
    table = jnp.concatenate(
        [weight_table(part, weight, count, whose, side, ndom, rows, donors) for whose in (dom, mate)], axis=0
    )

    edge = iota((cells, pitch), 0)
    for v in range(nv):
        u = x[v]
        below = jnp.where(edge == 0, 0.0, pltpu.roll(u, 1, 0))
        above = jnp.where(edge == cells - 1, 0.0, pltpu.roll(u, cells - 1, 0))
        upper = pltpu.roll(u, pitch - 1, 1)
        lower = pltpu.roll(u, 1, 1)
        base = 0.25 * (above + below + upper + lower - 4.0 * u) - speed[v] * (upper - lower) * 0.5
        res[v] = base
        res[v, :rows] = base[:rows] - 0.5 * u[:rows]

    line = spectral_line(ninst)
    half = ninst // 2
    even = [float(np.float32(0.5 * (line[j] + line[j + half]))) for j in range(half)]
    odd = [float(np.float32(0.5 * (line[j] - line[j + half]))) for j in range(half)]
    scale = -freq[0]

    def mix(g):
        v0, v1 = GROUPS[g]
        each(ninst, lambda k: forward_arrival(g, k).wait_recv())

        def tile(t, carry):
            v = v0 + t // (cut // 8)
            r = pl.multiple_of((t % (cut // 8)) * 8, 8)
            f = [fbuf[k, v, pl.ds(r, 8), :] for k in range(ninst)]
            e = [scale * (f[k] + f[k + half]) for k in range(half)]
            o = [scale * (f[k] - f[k + half]) for k in range(half)]
            for target in range(half):
                total_e = total_o = None
                for k in range(half):
                    j = target - k
                    ce = even[j % half]
                    co = odd[j] if j >= 0 else -odd[j + half]
                    total_e = ce * e[k] if total_e is None else total_e + ce * e[k]
                    total_o = co * o[k] if total_o is None else total_o + co * o[k]
                if target == 0:
                    back[v, pl.ds(pl.multiple_of(me * cut + r, 8), 8), :] = total_e + total_o
                else:
                    obuf[target, v, pl.ds(r, 8), :] = total_e + total_o
                obuf[target + half, v, pl.ds(r, 8), :] = total_e - total_o
            return carry

        lax.fori_loop(0, (v1 - v0) * (cut // 8), tile, 0)
        peers(lambda k: back_copy(g, k).start())

    def remap():
        each(nsite, lambda k: donor_arrival(k).wait_recv())
        for v in range(nv):
            arrived = jnp.concatenate([rbuf[i, v] for i in range(nsite)], axis=0)
            both = jnp.dot(table, arrived, precision=HIGHEST, preferred_element_type=jnp.float32)
            for n in range(2):
                for s in range(ninst):
                    at = n * rows + fine * s
                    mbuf[n, s, fine * v : fine * (v + 1)] = both[at : at + fine]
        peers(lambda k: mapped_copy(0, k).start())
        mapped_copy(1, 0).start()
        peers(lambda k: mapped_copy(1, k).start())
        mrec[0, 0] = mbuf[0, me]

    def interpolate():
        each(ninst, lambda k: mapped_arrival(0, k).wait_recv())
        mapped_arrival(1, 0).wait_recv()
        each(ninst, lambda k: mapped_arrival(1, k).wait_recv())
        mrec[0] = mrec[0] + mrec[1]

        def one(target, carry):
            total = wtab[target * ninst] * mrec[0, 0]
            for k in range(1, ninst):
                total = total + wtab[target * ninst + k] * mrec[0, k]
            gout[target] = total
            return carry

        lax.fori_loop(0, ninst, one, 0)
        peers(lambda k: ghost_copy(k).start())
        gback[me] = gout[0]

    remap()
    mix(0)
    interpolate()

    halo_copy(0).wait_recv()
    halo_copy(1).wait_recv()
    for v in range(nv):
        res[v, :1] = res[v, :1] + jnp.where(dom == 0, 0.0, 0.25 * hrecv[0, v])
        res[v, cells - 1 :] = res[v, cells - 1 :] + jnp.where(dom == ndom - 1, 0.0, 0.25 * hrecv[1, v])
    for g, (v0, v1) in enumerate(GROUPS):
        each(ninst, lambda k: back_arrival(g, k).wait_recv())
        for v in range(v0, v1):
            res[v] = res[v] + back[v]
    each(ninst, lambda k: ghost_arrival(k).wait_recv())
    for v in range(nv):
        full = jnp.concatenate([gback[s, fine * v : fine * (v + 1)] for s in range(ninst)], axis=0)
        ghost[v] = full
        res[v, :rows] = res[v, :rows] + 0.5 * full

    halo_copy(0).wait_send()
    halo_copy(1).wait_send()
    each(nsite, lambda k: donor_copy(k).wait_send())
    for g in range(len(GROUPS)):
        each(ninst, lambda k: forward_copy(g, k).wait_send())
        each(ninst, lambda k: back_copy(g, k).wait_send())
    each(ninst, lambda k: mapped_copy(0, k).wait_send())
    mapped_copy(1, 0).wait_send()
    each(ninst, lambda k: mapped_copy(1, k).wait_send())
    each(ninst, lambda k: ghost_copy(k).wait_send())


def place(res_in, ghost_in, res, ghost, sems):
    moves = [
        pltpu.make_async_copy(res_in, res, sems.at[0]),
        pltpu.make_async_copy(ghost_in, ghost, sems.at[1]),
    ]
    for move in moves:
        move.start()
    for move in moves:
        move.wait()


def solution(mesh):
    ninst, ndom = mesh.shape["inst"], mesh.shape["dom"]

    def body(flow_state, speed, freq, time_weights, shift, part, block, count, weight):
        x = flow_state[0]
        nv, cells, pitch = x.shape
        rows = part.shape[0] // ndom
        donors = part.shape[1]
        cap = rows * donors // ndom
        cut = cells // ninst
        fine = rows // ninst
        groups = len(GROUPS)
        hbm = pl.BlockSpec(memory_space=pltpu.HBM)
        vmem = pl.BlockSpec(memory_space=pltpu.VMEM)
        f32 = jnp.float32
        dma = pltpu.SemaphoreType.DMA
        given = (x, speed, freq, time_weights, shift, part.T, block.T, weight.T, count[None])
        given = [a if a.size == 1 else pltpu.with_memory_space_constraint(a, pltpu.HBM) for a in given]
        res, ghost = pl.pallas_call(
            functools.partial(kernel, ninst, ndom),
            out_shape=(pltpu.VMEM((nv, cells, pitch), f32), pltpu.VMEM((nv, rows, pitch), f32)),
            in_specs=[hbm] * 9,
            out_specs=(vmem, vmem),
            scratch_shapes=[
                pltpu.VMEM(x.shape, f32),
                pltpu.SMEM(speed.shape, f32),
                pltpu.SMEM(freq.shape, f32),
                pltpu.SMEM(time_weights.shape, f32),
                pltpu.SMEM(shift.shape, jnp.int32),
                pltpu.VMEM(part.T.shape, jnp.int32),
                pltpu.VMEM(part.T.shape, jnp.int32),
                pltpu.VMEM(part.T.shape, f32),
                pltpu.VMEM((1, count.shape[0]), jnp.int32),
                dma((9,)),
                pltpu.VMEM((ndom // 2, nv, 2 * cap, pitch), f32),
                pltpu.VMEM((ndom // 2, nv, 2 * cap, pitch), f32),
                pltpu.VMEM((ninst, nv, cut, pitch), f32),
                pltpu.VMEM((ninst, nv, cut, pitch), f32),
                pltpu.VMEM((nv, cells, pitch), f32),
                pltpu.VMEM((2, ninst, nv * fine, pitch), f32),
                pltpu.VMEM((2, ninst, nv * fine, pitch), f32),
                pltpu.VMEM((ninst, nv * fine, pitch), f32),
                pltpu.VMEM((ninst, nv * fine, pitch), f32),
                pltpu.VMEM((2, nv, 1, pitch), f32),
                pltpu.VMEM((2, nv, 1, pitch), f32),
                pltpu.SMEM((ninst * ninst,), f32),
                pltpu.SemaphoreType.REGULAR((1,)),
                dma((ndom // 2,)),
                dma((ndom // 2,)),
                dma((groups, ninst)),
                dma((groups, ninst)),
                dma((groups, ninst)),
                dma((groups, ninst)),
                dma((2, ninst)),
                dma((2, ninst)),
                dma((ninst,)),
                dma((ninst,)),
                dma((2,)),
                dma((2,)),
            ],
            compiler_params=pltpu.CompilerParams(
                collective_id=0, has_side_effects=True, vmem_limit_bytes=VMEM
            ),
            name="harmonic_residual",
        )(*given)
        res, ghost = pl.pallas_call(
            place,
            out_shape=(
                jax.ShapeDtypeStruct((nv, cells, pitch), f32),
                jax.ShapeDtypeStruct((nv, rows, pitch), f32),
            ),
            in_specs=[vmem, vmem],
            out_specs=(hbm, hbm),
            scratch_shapes=[dma((2,))],
            name="place_results",
        )(*(pltpu.with_memory_space_constraint(a, pltpu.VMEM) for a in (res, ghost)))
        return res[None], ghost[None]

    in_specs = (P("inst", None, "dom", None), P(), P(), P(), P(), P(), P(), P(), P())
    out_specs = (P("inst", None, "dom", None), P("inst", None, "dom", None))
    return jax.shard_map(body, mesh=mesh, in_specs=in_specs, out_specs=out_specs, check_vma=False)
```

```python
import functools

import jax
import jax.numpy as jnp
import numpy as np
from jax import lax
from jax.experimental import pallas as pl
from jax.experimental.pallas import tpu as pltpu
from jax.sharding import PartitionSpec as P

HIGHEST = lax.Precision.HIGHEST
VMEM = 32 << 20
MESH = pl.DeviceIdType.MESH
GROUPS = ((0, 5),)
ORDER = (12, 4, 8, 15, 3, 13, 1, 7, 11, 5, 9, 14, 6, 10, 2)


def spectral_line(length):
    j = np.arange(length)
    safe = np.where(j == 0, 1, j)
    line = 0.5 * np.where(j % 2 == 0, 1.0, -1.0) / np.tan(np.pi * safe / length)
    return np.where(j == 0, -2.0, line) + 2.0 / length


def iota(shape, dim):
    return lax.broadcasted_iota(jnp.int32, shape, dim)


def send_table(part_ref, block_ref, dom, ndom, rows, donors):
    lanes = 128
    chunks = ndom * rows // lanes
    parts = jnp.concatenate([part_ref[:, lanes * g : lanes * (g + 1)] for g in range(chunks)], axis=0)
    blocks = jnp.concatenate([block_ref[:, lanes * g : lanes * (g + 1)] for g in range(chunks)], axis=0)
    count = chunks * donors
    cap = rows * donors // ndom
    per = lanes // rows
    wanted = parts == dom
    ones = jnp.where(wanted, 1.0, 0.0)
    a, b = iota((lanes, lanes), 0), iota((lanes, lanes), 1)
    same = (a // rows) == (b // rows)
    before = jnp.where(same & (a < b), 1.0, 0.0)
    whole = jnp.where(same, 1.0, 0.0)
    ra, rb = iota((count, count), 0), iota((count, count), 1)
    lower = jnp.where(((ra // donors) == (rb // donors)) & (rb < ra), 1.0, 0.0)
    dot = functools.partial(jnp.dot, preferred_element_type=jnp.float32)
    rank = dot(ones, before) + dot(lower, dot(ones, whole))
    total = jnp.zeros((count, lanes), jnp.float32)
    values = blocks.astype(jnp.float32)
    for c in range(cap):
        picked = jnp.where(wanted & (rank == float(c)), values, 0.0)
        group = a // rows
        spread = jnp.where((b % (per * cap)) == ((group % 2) * 2 + group // 2) * cap + c, 1.0, 0.0)
        total = total + dot(picked, spread)
    row, lane = iota((count, lanes), 0), iota((count, lanes), 1)
    line = jnp.sum(
        jnp.where((lane // (per * cap)) == (row // donors), total, 0.0), axis=0, keepdims=True
    )
    return jnp.transpose(jnp.broadcast_to(line, (lanes, lanes)))


def weight_table(part_ref, weight_ref, count_ref, dom, side, ndom, rows, donors):
    lanes = 128
    per = lanes // rows
    cap = rows * donors // ndom
    at = pl.ds(pl.multiple_of((dom // per) * lanes, lanes), lanes)
    own = jnp.concatenate(
        [
            part_ref[:, at].astype(jnp.float32),
            weight_ref[:, at],
            jnp.broadcast_to(count_ref[:, at].astype(jnp.float32), (8, lanes)),
        ],
        axis=0,
    )
    a, b = iota((lanes, lanes), 0), iota((lanes, lanes), 1)
    pick = jnp.where(a == (dom % per) * rows + b % rows, 1.0, 0.0)
    own = jnp.dot(own, pick, precision=HIGHEST, preferred_element_type=jnp.float32)
    row, lane = iota((donors, lanes), 0), iota((donors, lanes), 1)
    mine = (lane // rows) == row
    part = jnp.sum(jnp.where(mine, own[:donors], 0.0), axis=0, keepdims=True)
    live = mine & (row.astype(jnp.float32) < own[2 * donors : 3 * donors])
    weight = jnp.sum(jnp.where(live, own[donors : 2 * donors], 0.0), axis=0, keepdims=True)
    part_row = jnp.broadcast_to(part, (lanes, lanes))
    part_col = jnp.transpose(part_row)
    rank = jnp.sum(jnp.where((part_row == part_col) & (a < b), 1.0, 0.0), axis=0, keepdims=True)
    named = part.astype(jnp.int32)
    site = (named // 4) * 2 + named % 2
    slot = (site * 2 + (dom // 2) % 2).astype(jnp.float32) * cap + rank
    slot = jnp.where((named // 2) % 2 == side, slot, -1.0)
    slot_col = jnp.transpose(jnp.broadcast_to(slot, (lanes, lanes)))
    weight_col = jnp.transpose(jnp.broadcast_to(weight, (lanes, lanes)))
    spread = jnp.where(slot_col == b.astype(jnp.float32), weight_col, 0.0)
    top = sum(spread[rows * k : rows * (k + 1)] for k in range(donors))
    bottom = sum(weight_col[rows * k : rows * (k + 1)] for k in range(donors))
    return top / bottom


def kernel(
    ninst,
    ndom,
    x_in,
    speed_in,
    freq_in,
    time_weights_in,
    shift_in,
    part_in,
    block_in,
    weight_in,
    count_in,
    res,
    ghost,
    x,
    speed,
    freq,
    time_weights,
    shift,
    part,
    block,
    weight,
    count,
    loads,
    sbuf,
    rbuf,
    fbuf,
    obuf,
    back,
    mbuf,
    mrec,
    gout,
    gback,
    hsend,
    hrecv,
    wtab,
    go,
    d_send,
    d_recv,
    f_send,
    f_recv,
    b_send,
    b_recv,
    m_send,
    m_recv,
    g_send,
    g_recv,
    h_send,
    h_recv,
):
    nv, cells, pitch = x.shape
    rows = ghost.shape[1]
    donors = part.shape[0]
    cap = rows * donors // ndom
    cut = cells // ninst
    fine = rows // ninst
    me, dom = lax.axis_index("inst"), lax.axis_index("dom")

    def inst_of(k):
        return lax.rem(me + k, ninst)

    def dom_of(k):
        return lax.rem(dom + k, ndom)

    nsite = ndom // 2
    side = (dom // 2) % 2
    site = (dom // 4) * 2 + dom % 2
    mate = dom + 2 - 4 * side
    core = dom % 2
    depth = ndom // 4
    layer = dom // 4

    def first_core_at(z, s):
        return lax.rem(z + depth, depth) * 4 + s * 2

    def site_of(k):
        return lax.rem(site + k, nsite)

    def dom_at(i):
        return (i // 2) * 4 + side * 2 + i % 2

    def own_rows(i):
        return pl.ds(pl.multiple_of(i * cut, cut), cut)

    def remote(src, dst, send, recv, to):
        return pltpu.make_async_remote_copy(
            src_ref=src, dst_ref=dst, send_sem=send, recv_sem=recv, device_id=to, device_id_type=MESH
        )

    def donor_copy(k):
        to = site_of(k)
        return remote(sbuf.at[to], rbuf.at[site], d_send.at[k], d_recv.at[nsite - k], (me, dom_at(to)))

    def donor_arrival(k):
        return remote(sbuf.at[0], rbuf.at[site_of(k)], d_send.at[k], d_recv.at[k], (me, dom_at(site_of(k))))

    def forward_copy(g, k):
        v0, v1 = GROUPS[g]
        to = inst_of(k)
        return remote(
            x.at[v0:v1, own_rows(to)],
            fbuf.at[ninst - k, v0:v1],
            f_send.at[g, k],
            f_recv.at[g, ninst - k],
            (to, dom),
        )

    def forward_arrival(g, k):
        v0, v1 = GROUPS[g]
        return remote(
            x.at[v0:v1, own_rows(me)], fbuf.at[k, v0:v1], f_send.at[g, k], f_recv.at[g, k], (inst_of(k), dom)
        )

    def back_copy(g, k):
        v0, v1 = GROUPS[g]
        return remote(
            obuf.at[k, v0:v1],
            back.at[v0:v1, own_rows(me)],
            b_send.at[g, k],
            b_recv.at[g, ninst - k],
            (inst_of(k), dom),
        )

    def back_arrival(g, k):
        v0, v1 = GROUPS[g]
        return remote(
            obuf.at[k, v0:v1], back.at[v0:v1, own_rows(inst_of(k))], b_send.at[g, k], b_recv.at[g, k], (inst_of(k), dom)
        )

    def mapped_copy(n, k):
        to, slot = inst_of(k), (ninst - k) % ninst
        return remote(
            mbuf.at[n, to], mrec.at[n, slot], m_send.at[n, k], m_recv.at[n, slot], (to, mate if n else dom)
        )

    def mapped_arrival(n, k):
        return remote(
            mbuf.at[n, 0], mrec.at[n, k], m_send.at[n, k], m_recv.at[n, k], (inst_of(k), mate if n else dom)
        )

    def ghost_copy(k):
        return remote(gout.at[k], gback.at[me], g_send.at[k], g_recv.at[ninst - k], (inst_of(k), dom))

    def ghost_arrival(k):
        return remote(gout.at[k], gback.at[inst_of(k)], g_send.at[k], g_recv.at[k], (inst_of(k), dom))

    def halo_copy(side):
        to = dom_of(1 if side == 0 else ndom - 1)
        return remote(hsend.at[side], hrecv.at[side], h_send.at[side], h_recv.at[side], (me, to))

    def each(count, act):
        def step(k, carry):
            act(k)
            return carry

        lax.fori_loop(1, count, step, 0)

    def peers(act):
        for k in ORDER:
            act(k)

    def far_peers(act):
        for k in reversed(ORDER):
            act(k)

    def sites(act):
        def step(t, carry):
            act(nsite // 2 + (1 - 2 * lax.rem(t, 2)) * ((t + 1) // 2))
            return carry

        lax.fori_loop(0, nsite - 1, step, 0)

    barrier = pltpu.get_barrier_semaphore()

    def greet(to):
        pl.semaphore_signal(barrier, inc=1, device_id=to, device_id_type=MESH)

    peers(lambda k: greet((inst_of(k), dom)))

    @pl.when(core == 1)
    def _():
        greet((me, dom - 1))

    for k in range(1, depth):
        greet((me, first_core_at(layer + k, side)))
    greet((me, first_core_at(layer - 1 + 2 * side, 1 - side)))
    for k in (0, *ORDER):
        greet((inst_of(k), first_core_at(layer, 1 - side)))

    pairs = (
        (x_in, x),
        (part_in, part),
        (block_in, block),
        (speed_in, speed),
        (freq_in, freq),
        (time_weights_in, time_weights),
        (shift_in, shift),
        (weight_in, weight),
        (count_in, count),
    )
    arriving = [pltpu.make_async_copy(a, b, loads.at[n]) for n, (a, b) in enumerate(pairs)]
    for load in arriving:
        load.start()

    for load in arriving:
        load.wait()
    column = send_table(part, block, dom, ndom, rows, donors)
    lane = iota(column.shape, 1).astype(jnp.float32)
    chosen = jnp.concatenate(
        [jnp.where(column == lane + float(s), 1.0, 0.0) for s in range(0, cells, 128)], axis=1
    )
    for v in range(nv):
        out = jnp.dot(chosen, x[v], precision=HIGHEST, preferred_element_type=jnp.float32)
        for i in range(nsite):
            sbuf[i, v] = out[i * 2 * cap : (i + 1) * 2 * cap]
        hsend[0, v] = x[v, cells - 1 :, :]
        hsend[1, v] = x[v, :1, :]

    @pl.when(core == 1)
    def _():
        pl.semaphore_wait(barrier, ninst - 1)

    @pl.when(core == 0)
    def _():
        pl.semaphore_wait(barrier, ninst - 1 + 1 + 2 * (depth - 1) + 2 + 2 * ninst)
        pl.semaphore_signal(go.at[0], inc=1, device_id=(me, dom + 1), device_id_type=MESH)

    def forward():
        for g in range(len(GROUPS)):
            peers(lambda k: forward_copy(g, k).start())

    @pl.when(core == 0)
    def _():
        sites(lambda k: donor_copy(k).start())
        forward()

    @pl.when(core == 1)
    def _():
        forward()
        pl.semaphore_wait(go.at[0], 1)
        sites(lambda k: donor_copy(k).start())

    halo_copy(0).start()
    halo_copy(1).start()

    rbuf[site] = sbuf[site]
    for v in range(nv):
        fbuf[0, v] = x[v, own_rows(me), :]

    def weights_of(target, carry):
        phase = shift[inst_of(target)]
        for k in range(ninst):
            wtab[target * ninst + k] = time_weights[jnp.bitwise_and(me + k - phase, ninst - 1)]
        return carry

    lax.fori_loop(0, ninst, weights_of, 0)
    table = jnp.concatenate(
        [weight_table(part, weight, count, whose, side, ndom, rows, donors) for whose in (dom, mate)], axis=0
    )

    edge = iota((cells, pitch), 0)
    for v in range(nv):
        u = x[v]
        below = jnp.where(edge == 0, 0.0, pltpu.roll(u, 1, 0))
        above = jnp.where(edge == cells - 1, 0.0, pltpu.roll(u, cells - 1, 0))
        upper = pltpu.roll(u, pitch - 1, 1)
        lower = pltpu.roll(u, 1, 1)
        base = 0.25 * (above + below + upper + lower - 4.0 * u) - speed[v] * (upper - lower) * 0.5
        res[v] = base
        res[v, :rows] = base[:rows] - 0.5 * u[:rows]

    line = spectral_line(ninst)
    half = ninst // 2
    even = [float(np.float32(0.5 * (line[j] + line[j + half]))) for j in range(half)]
    odd = [float(np.float32(0.5 * (line[j] - line[j + half]))) for j in range(half)]
    scale = -freq[0]

    def mix(g):
        v0, v1 = GROUPS[g]
        each(ninst, lambda k: forward_arrival(g, k).wait_recv())

        def tile(t, carry):
            v = v0 + t // (cut // 8)
            r = pl.multiple_of((t % (cut // 8)) * 8, 8)
            f = [fbuf[k, v, pl.ds(r, 8), :] for k in range(ninst)]
            e = [scale * (f[k] + f[k + half]) for k in range(half)]
            o = [scale * (f[k] - f[k + half]) for k in range(half)]
            for target in range(half):
                total_e = total_o = None
                for k in range(half):
                    j = target - k
                    ce = even[j % half]
                    co = odd[j] if j >= 0 else -odd[j + half]
                    total_e = ce * e[k] if total_e is None else total_e + ce * e[k]
                    total_o = co * o[k] if total_o is None else total_o + co * o[k]
                if target == 0:
                    back[v, pl.ds(pl.multiple_of(me * cut + r, 8), 8), :] = total_e + total_o
                else:
                    obuf[target, v, pl.ds(r, 8), :] = total_e + total_o
                obuf[target + half, v, pl.ds(r, 8), :] = total_e - total_o
            return carry

        lax.fori_loop(0, (v1 - v0) * (cut // 8), tile, 0)
        peers(lambda k: back_copy(g, k).start())

    def remap():
        each(nsite, lambda k: donor_arrival(k).wait_recv())
        for v in range(nv):
            arrived = jnp.concatenate([rbuf[i, v] for i in range(nsite)], axis=0)
            both = jnp.dot(table, arrived, precision=HIGHEST, preferred_element_type=jnp.float32)
            for n in range(2):
                for s in range(ninst):
                    at = n * rows + fine * s
                    mbuf[n, s, fine * v : fine * (v + 1)] = both[at : at + fine]
        far_peers(lambda k: mapped_copy(0, k).start())
        mapped_copy(1, 0).start()
        far_peers(lambda k: mapped_copy(1, k).start())
        mrec[0, 0] = mbuf[0, me]

    def interpolate():
        each(ninst, lambda k: mapped_arrival(0, k).wait_recv())
        mapped_arrival(1, 0).wait_recv()
        each(ninst, lambda k: mapped_arrival(1, k).wait_recv())
        mrec[0] = mrec[0] + mrec[1]

        def one(target, carry):
            total = wtab[target * ninst] * mrec[0, 0]
            for k in range(1, ninst):
                total = total + wtab[target * ninst + k] * mrec[0, k]
            gout[target] = total
            return carry

        lax.fori_loop(0, ninst, one, 0)
        far_peers(lambda k: ghost_copy(k).start())
        gback[me] = gout[0]

    remap()
    mix(0)
    interpolate()

    halo_copy(0).wait_recv()
    halo_copy(1).wait_recv()
    for v in range(nv):
        res[v, :1] = res[v, :1] + jnp.where(dom == 0, 0.0, 0.25 * hrecv[0, v])
        res[v, cells - 1 :] = res[v, cells - 1 :] + jnp.where(dom == ndom - 1, 0.0, 0.25 * hrecv[1, v])
    for g, (v0, v1) in enumerate(GROUPS):
        each(ninst, lambda k: back_arrival(g, k).wait_recv())
        for v in range(v0, v1):
            res[v] = res[v] + back[v]
    each(ninst, lambda k: ghost_arrival(k).wait_recv())
    for v in range(nv):
        full = jnp.concatenate([gback[s, fine * v : fine * (v + 1)] for s in range(ninst)], axis=0)
        ghost[v] = full
        res[v, :rows] = res[v, :rows] + 0.5 * full

    halo_copy(0).wait_send()
    halo_copy(1).wait_send()
    each(nsite, lambda k: donor_copy(k).wait_send())
    for g in range(len(GROUPS)):
        each(ninst, lambda k: forward_copy(g, k).wait_send())
        each(ninst, lambda k: back_copy(g, k).wait_send())
    each(ninst, lambda k: mapped_copy(0, k).wait_send())
    mapped_copy(1, 0).wait_send()
    each(ninst, lambda k: mapped_copy(1, k).wait_send())
    each(ninst, lambda k: ghost_copy(k).wait_send())


def place(res_in, ghost_in, res, ghost, sems):
    moves = [
        pltpu.make_async_copy(res_in, res, sems.at[0]),
        pltpu.make_async_copy(ghost_in, ghost, sems.at[1]),
    ]
    for move in moves:
        move.start()
    for move in moves:
        move.wait()


def solution(mesh):
    ninst, ndom = mesh.shape["inst"], mesh.shape["dom"]

    def body(flow_state, speed, freq, time_weights, shift, part, block, count, weight):
        x = flow_state[0]
        nv, cells, pitch = x.shape
        rows = part.shape[0] // ndom
        donors = part.shape[1]
        cap = rows * donors // ndom
        cut = cells // ninst
        fine = rows // ninst
        groups = len(GROUPS)
        hbm = pl.BlockSpec(memory_space=pltpu.HBM)
        vmem = pl.BlockSpec(memory_space=pltpu.VMEM)
        f32 = jnp.float32
        dma = pltpu.SemaphoreType.DMA
        given = (x, speed, freq, time_weights, shift, part.T, block.T, weight.T, count[None])
        given = [a if a.size == 1 else pltpu.with_memory_space_constraint(a, pltpu.HBM) for a in given]
        res, ghost = pl.pallas_call(
            functools.partial(kernel, ninst, ndom),
            out_shape=(pltpu.VMEM((nv, cells, pitch), f32), pltpu.VMEM((nv, rows, pitch), f32)),
            in_specs=[hbm] * 9,
            out_specs=(vmem, vmem),
            scratch_shapes=[
                pltpu.VMEM(x.shape, f32),
                pltpu.SMEM(speed.shape, f32),
                pltpu.SMEM(freq.shape, f32),
                pltpu.SMEM(time_weights.shape, f32),
                pltpu.SMEM(shift.shape, jnp.int32),
                pltpu.VMEM(part.T.shape, jnp.int32),
                pltpu.VMEM(part.T.shape, jnp.int32),
                pltpu.VMEM(part.T.shape, f32),
                pltpu.VMEM((1, count.shape[0]), jnp.int32),
                dma((9,)),
                pltpu.VMEM((ndom // 2, nv, 2 * cap, pitch), f32),
                pltpu.VMEM((ndom // 2, nv, 2 * cap, pitch), f32),
                pltpu.VMEM((ninst, nv, cut, pitch), f32),
                pltpu.VMEM((ninst, nv, cut, pitch), f32),
                pltpu.VMEM((nv, cells, pitch), f32),
                pltpu.VMEM((2, ninst, nv * fine, pitch), f32),
                pltpu.VMEM((2, ninst, nv * fine, pitch), f32),
                pltpu.VMEM((ninst, nv * fine, pitch), f32),
                pltpu.VMEM((ninst, nv * fine, pitch), f32),
                pltpu.VMEM((2, nv, 1, pitch), f32),
                pltpu.VMEM((2, nv, 1, pitch), f32),
                pltpu.SMEM((ninst * ninst,), f32),
                pltpu.SemaphoreType.REGULAR((1,)),
                dma((ndom // 2,)),
                dma((ndom // 2,)),
                dma((groups, ninst)),
                dma((groups, ninst)),
                dma((groups, ninst)),
                dma((groups, ninst)),
                dma((2, ninst)),
                dma((2, ninst)),
                dma((ninst,)),
                dma((ninst,)),
                dma((2,)),
                dma((2,)),
            ],
            compiler_params=pltpu.CompilerParams(
                collective_id=0, has_side_effects=True, vmem_limit_bytes=VMEM
            ),
            name="harmonic_residual",
        )(*given)
        res, ghost = pl.pallas_call(
            place,
            out_shape=(
                jax.ShapeDtypeStruct((nv, cells, pitch), f32),
                jax.ShapeDtypeStruct((nv, rows, pitch), f32),
            ),
            in_specs=[vmem, vmem],
            out_specs=(hbm, hbm),
            scratch_shapes=[dma((2,))],
            name="place_results",
        )(*(pltpu.with_memory_space_constraint(a, pltpu.VMEM) for a in (res, ghost)))
        return res[None], ghost[None]

    in_specs = (P("inst", None, "dom", None), P(), P(), P(), P(), P(), P(), P(), P())
    out_specs = (P("inst", None, "dom", None), P("inst", None, "dom", None))
    return jax.shard_map(body, mesh=mesh, in_specs=in_specs, out_specs=out_specs, check_vma=False)
```
